256 devices in a mesh: row: 16 (over z, core), col: 16 (over x, y).
Axes of the slice: x: 4, y: 4, z: 8, core: 2. Of those that a mesh axis runs over, the one named last changes fastest.
Arguments:
- start_panel: bfloat16 [262144, 128], P(('col', 'row')), may hold values from -6 to 6
- block_values: bfloat16 [16, 16, 352, 128, 128], P('row', 'col'), may hold values from -0.078125 to 0.078125
- block_rows: int32 [16, 16, 352], P('row', 'col'), may hold values from 0 to 127, as said below
- block_cols: int32 [16, 16, 352], P('row', 'col'), may hold values from 0 to 127, as said below
- block_counts: int32 [16, 16], P('row', 'col'), may hold values from 141 to 352, as said below
Outputs:
- left_panel: bfloat16 [262144, 128], P(('row', 'col'))
- right_panel: bfloat16 [262144, 128], P(('col', 'row'))
The draws below stay inside these ranges and needn't reach their ends.
Inputs may be any that keep to these rules, and one draw needn't show every extreme that they name: `block_rows`: block rows lie in 0 to 127 within each tile; low block rows hold more blocks; in every tile some live slot names block row 127. `block_cols`: in every tile some live slot names block column 127; a position may repeat. Only the first block_counts[r, c] slots of tile (r, c) are live; some tile fills all 352 slots.
All inputs are finite; a program needn't handle non-finite values.
Results may differ from the reference program's by a relative error of at most 0.0085.
Values may be sent and summed in bfloat16 or wider, within the bound.
A program may use at most 128 MiB of HBM per device.

```python
import jax
import jax.numpy as jnp
from jax import lax

BLK = 128
PANEL = 128
GROUP = 1024
KB = 352
NODES = 262144
BR = 128
BC = 128
N_ROW = 16
N_COL = 16


def draw_block_rows(key, part):
    first, second, third = jax.random.split(jax.random.fold_in(key, 11), 3)
    shape = (N_ROW, N_COL, KB)
    left = jax.random.randint(first, shape, 0, BR, dtype=jnp.int32)
    right = jax.random.randint(second, shape, 0, BR, dtype=jnp.int32)
    rows_drawn = left * right // BR
    placed = jax.random.randint(third, (N_ROW, N_COL, 1), 0, KB - 3 * KB // 5, dtype=jnp.int32)
    slots = jnp.arange(KB, dtype=jnp.int32)[None, None, :]
    return jnp.where(slots == placed, BR - 1, rows_drawn).astype(jnp.int32)


def draw_block_cols(key, part):
    first, third = jax.random.split(jax.random.fold_in(key, 23), 2)
    cols_drawn = jax.random.randint(first, (N_ROW, N_COL, KB), 0, BC, dtype=jnp.int32)
    placed = jax.random.randint(third, (N_ROW, N_COL, 1), 0, KB - 3 * KB // 5, dtype=jnp.int32)
    slots = jnp.arange(KB, dtype=jnp.int32)[None, None, :]
    return jnp.where(slots == placed, BC - 1, cols_drawn).astype(jnp.int32)


def draw_block_counts(key, part):
    first, second = jax.random.split(jax.random.fold_in(key, 37), 2)
    counts_drawn = KB - jax.random.randint(first, (N_ROW, N_COL), 0, 3 * KB // 5 + 1, dtype=jnp.int32)
    fullest = jax.random.randint(second, (), 0, N_ROW * N_COL, dtype=jnp.int32)
    tiles = jnp.arange(N_ROW * N_COL, dtype=jnp.int32).reshape(N_ROW, N_COL)
    return jnp.where(tiles == fullest, KB, counts_drawn).astype(jnp.int32)


def levels(own_key, extent, shards, least, largest):
    loudness = 1.0
    for position, shards_of in shards:
        steps = jax.random.uniform(jax.random.fold_in(jax.random.fold_in(own_key, 6), position), (shards_of,), jnp.float32, least / len(shards), largest / len(shards))
        loudness = loudness * jnp.repeat(jnp.exp(steps), extent[position] // shards_of).reshape((-1,) + (1,) * (len(extent) - 1 - position))
    return loudness


def normal_values(rng, dims, width, limit, cuts=(), kind=jnp.bfloat16):
    entries = width * jax.random.normal(rng, dims, jnp.float32)
    if cuts:
        entries = entries * levels(rng, dims, cuts, -0.22, 0.18)
    return jnp.clip(entries, -limit, limit).astype(kind)


def setup_inputs(seed: int = 0) -> dict:
    seeds = jax.random.split(jax.random.key(seed), 6)
    start_panel = normal_values(seeds[0], (NODES, PANEL), 1.0, 6.0, ((0, 256),))
    block_values = normal_values(seeds[1], (N_ROW, N_COL, KB, BLK, BLK), (KB * N_COL * BLK // BR) ** -0.5, 0.078125, ((0, 16), (1, 16)))
    block_rows = draw_block_rows(jax.random.fold_in(seeds[5], 71), 0)
    block_cols = draw_block_cols(jax.random.fold_in(seeds[5], 71), 0)
    block_counts = draw_block_counts(jax.random.fold_in(seeds[5], 71), 0)
    return dict(start_panel=start_panel, block_values=block_values, block_rows=block_rows, block_cols=block_cols, block_counts=block_counts)


def tile_product(values, index_out, index_in, live_count, panel_in, out_blocks, flipped):
    block_size = values.shape[-1]
    pieces = panel_in.reshape(-1, block_size, panel_in.shape[1])
    selected = jnp.take(pieces, index_in, axis=0).astype(jnp.float32)
    if flipped:
        products = jnp.einsum('kij,kip->kjp', values.astype(jnp.float32), selected)
    else:
        products = jnp.einsum('kij,kjp->kip', values.astype(jnp.float32), selected)
    live = (jnp.arange(values.shape[0]) < live_count).astype(jnp.float32)
    products = products * live[:, None, None]
    summed = jax.ops.segment_sum(products, index_out, num_segments=out_blocks)
    return summed.reshape(out_blocks * block_size, panel_in.shape[1])

def lower_cholesky(gram_total):
    order = gram_total.shape[0]
    positions = jnp.arange(order, dtype=jnp.int32)

    def column_step(index, lower):
        row_of = lax.dynamic_slice_in_dim(lower, index, 1, 0)[0]
        column = lax.dynamic_slice_in_dim(gram_total, index, 1, 1)[:, 0]
        column = column - jnp.dot(lower, row_of, precision=lax.Precision.HIGHEST)
        pivot = jnp.sqrt(lax.dynamic_slice_in_dim(column, index, 1, 0)[0])
        column = jnp.where(positions >= index, column / pivot, jnp.zeros_like(column))
        return lax.dynamic_update_slice_in_dim(lower, column[:, None], index, 1)
    return lax.fori_loop(0, order, column_step, jnp.zeros_like(gram_total))

def lower_inverse(lower):
    order = lower.shape[0]
    positions = jnp.arange(order, dtype=jnp.int32)

    def row_step(index, inverse):
        row_of = lax.dynamic_slice_in_dim(lower, index, 1, 0)[0]
        pivot = lax.dynamic_slice_in_dim(row_of, index, 1, 0)[0]
        unit = (positions == index).astype(lower.dtype)
        new_row = (unit - jnp.dot(row_of, inverse, precision=lax.Precision.HIGHEST)) / pivot
        return lax.dynamic_update_slice_in_dim(inverse, new_row[None, :], index, 0)
    return lax.fori_loop(0, order, row_step, jnp.zeros_like(lower))

def apply_factor(y_rounded, gram_total):
    inverse = lower_inverse(lower_cholesky(gram_total))
    solved = jnp.dot(y_rounded.astype(jnp.float32), inverse.T, precision=lax.Precision.HIGHEST)
    return solved.astype(jnp.bfloat16)

def reference(start_panel, block_values, block_rows, block_cols, block_counts):
    nodes_total = GROUP * N_ROW * N_COL
    row_tile = GROUP * N_COL
    col_tile = GROUP * N_ROW
    tiles = jnp.arange(N_ROW * N_COL, dtype=jnp.int32)

    def left_step(carry, tile_id):
        rowidx = (tile_id // N_COL).astype(jnp.int32)
        colidx = (tile_id % N_COL).astype(jnp.int32)
        panel_in = lax.dynamic_slice_in_dim(start_panel, colidx * col_tile, col_tile, 0)
        added = tile_product(block_values[rowidx, colidx], block_rows[rowidx, colidx], block_cols[rowidx, colidx], block_counts[rowidx, colidx], panel_in, BR, False)
        current = lax.dynamic_slice_in_dim(carry, rowidx * row_tile, row_tile, 0)
        return (lax.dynamic_update_slice_in_dim(carry, current + added, rowidx * row_tile, 0), None)
    left_sum, _ = lax.scan(left_step, jnp.zeros((nodes_total, PANEL), jnp.float32), tiles)
    left_y = left_sum.astype(jnp.bfloat16)
    left_gram = jnp.dot(left_y.T, left_y, preferred_element_type=jnp.float32) / nodes_total
    left_panel = apply_factor(left_y, left_gram)

    def right_step(carry, tile_id):
        rowidx = (tile_id // N_COL).astype(jnp.int32)
        colidx = (tile_id % N_COL).astype(jnp.int32)
        panel_in = lax.dynamic_slice_in_dim(left_panel, rowidx * row_tile, row_tile, 0)
        added = tile_product(block_values[rowidx, colidx], block_cols[rowidx, colidx], block_rows[rowidx, colidx], block_counts[rowidx, colidx], panel_in, BC, True)
        current = lax.dynamic_slice_in_dim(carry, colidx * col_tile, col_tile, 0)
        return (lax.dynamic_update_slice_in_dim(carry, current + added, colidx * col_tile, 0), None)
    right_sum, _ = lax.scan(right_step, jnp.zeros((nodes_total, PANEL), jnp.float32), tiles)
    right_y = right_sum.astype(jnp.bfloat16)
    right_gram = jnp.dot(right_y.T, right_y, preferred_element_type=jnp.float32) / nodes_total
    right_panel = apply_factor(right_y, right_gram)
    return (left_panel, right_panel)
```

```python
import functools

import jax
import jax.numpy as jnp
from jax import lax
from jax.experimental import pallas as pl
from jax.experimental.pallas import tpu as pltpu
from jax.sharding import PartitionSpec as P

MESH = pl.DeviceIdType.MESH
F32 = jnp.float32
BF16 = jnp.bfloat16
HIGHEST = lax.Precision.HIGHEST

H = 2
PH = 64
NZ = 8
UNROLL = 16
SENDS = 320


class Copies:
    def __init__(self, send_sems, recv_sems):
        self.send_sems, self.recv_sems = send_sems, recv_sems
        self.index, self.sent = {}, []

    def sems(self, name):
        number = self.index.setdefault(name, len(self.index))
        assert number < SENDS
        return self.send_sems.at[number], self.recv_sems.at[number]

    def make(self, name, src, dst, device):
        send, recv = self.sems(name)
        return pltpu.make_async_remote_copy(
            src_ref=src, dst_ref=dst, send_sem=send, recv_sem=recv, device_id=device, device_id_type=MESH
        )

    def send(self, name, src, dst, device):
        copy = self.make(name, src, dst, device)
        copy.start()
        self.sent.append(copy)

    def arrived(self, name, dst, device):
        self.make(name, dst, dst, device).wait_recv()

    def drain(self):
        for copy in self.sent:
            copy.wait_send()
        self.sent = []


def factor_inverse(gram_ref, work, inv):
    n = gram_ref.shape[0]
    lanes = lax.broadcasted_iota(jnp.int32, (8, n), 1)
    subs = lax.broadcasted_iota(jnp.int32, (8, n), 0)
    work[...] = gram_ref[...]
    rows = lax.broadcasted_iota(jnp.int32, (n, n), 0)
    cols = lax.broadcasted_iota(jnp.int32, (n, n), 1)
    inv[...] = jnp.where(rows == cols, 1.0, 0.0).astype(F32)

    def block(jb, carry):
        start = pl.multiple_of(jb * 8, 8)
        d = pltpu.roll(work[pl.ds(start, 8), :], lax.rem(n - start, n), 1)
        m = inv[pl.ds(start, 8), :]
        scale = jnp.zeros((8, n), F32)
        for i in range(8):
            pivot = jnp.broadcast_to(d[i : i + 1, i : i + 1], (8, n))
            column = jnp.broadcast_to(d[:, i : i + 1], (8, n))
            factor = jnp.where(subs > i, column / pivot, 0.0)
            scale = jnp.where(subs == i, pivot, scale)
            d = d - factor * d[i : i + 1, :]
            m = m - factor * m[i : i + 1, :]
        d = pltpu.roll(d, start, 1)
        multipliers = jnp.where(lanes >= start + 8, d / scale, 0.0)
        work[...] = work[...] - lax.dot_general(
            multipliers, d, (((0,), (0,)), ((), ())), precision=HIGHEST, preferred_element_type=F32
        )
        inv[...] = inv[...] - lax.dot_general(
            multipliers, m, (((0,), (0,)), ((), ())), precision=HIGHEST, preferred_element_type=F32
        )
        inv[pl.ds(start, 8), :] = m / jnp.sqrt(scale)
        return carry

    lax.fori_loop(0, n // 8, block, 0)


def kernel(
    nodes_total,
    codes,
    keeps,
    lasts,
    start_ref,
    values_hbm,
    left_out,
    right_out,
    values,
    gathered,
    sums,
    partial,
    partial2,
    relay1,
    full1,
    mid,
    mid_own,
    relay2,
    full2,
    left_all,
    left_y,
    pair_in,
    ring_out,
    ring_in,
    z_sum,
    right_y,
    gram_part,
    gram_in1,
    gram_slice,
    gram_in2,
    gram_total,
    work,
    inv1,
    inv2,
    local_sem,
    send_sems,
    recv_sems,
):
    slots = values_hbm.shape[0]
    r = lax.axis_index("row")
    c = lax.axis_index("col")
    z, core = r // 2, lax.rem(r, 2)
    position = {"x": c // 4, "y": lax.rem(c, 4)}
    x, y = position["x"], position["y"]
    sibling = {"row": 2 * z + 1 - core}
    z_next = ({"row": lax.rem(r + 2, 16)}, {"row": lax.rem(r + 14, 16)})
    nearby = {
        "x": ({"col": lax.rem(c + 4, 16)}, {"col": lax.rem(c + 12, 16)}),
        "y": ({"col": 4 * x + lax.rem(y + 1, 4)}, {"col": 4 * x + lax.rem(y + 3, 4)}),
    }
    axes = (("x", "y"), ("y", "x"))
    copies = Copies(send_sems, recv_sems)
    chunks = [(h, path) for h in range(H) for path in range(2)]

    load_values = pltpu.make_async_copy(values_hbm, values, local_sem)
    load_values.start()

    barrier = pltpu.get_barrier_semaphore()
    for t in range(1, 16):
        pl.semaphore_signal(barrier, inc=1, device_id={"row": lax.rem(r + t, 16)}, device_id_type=MESH)
        pl.semaphore_signal(barrier, inc=1, device_id={"col": lax.rem(c + t, 16)}, device_id_type=MESH)

    for b in range(8):
        turned = start_ref[128 * b : 128 * b + 128, :].astype(F32).T.astype(BF16)
        for h in range(H):
            gathered[h, r * 8 + b] = turned[PH * h : PH * h + PH, :]
    sums[slots] = jnp.zeros((128, 128), BF16)
    pl.semaphore_wait(barrier, 30)

    def group(h, number, first=0, count=8):
        return gathered.at[h, pl.ds(number * 8 + first, count)]

    for h in range(H):
        own = group(h, r)
        for way in range(2):
            copies.send(("gz", h, way, 1), own, own, z_next[way])
    for h in range(H):
        own = group(h, r)
        copies.send(("gs", h, 0, 0), own, own, sibling)

    def origin(way, s):
        return lax.rem(r + (32 - 2 * s if way == 0 else 2 * s), 16)

    def origin_sibling(way, s):
        return lax.rem(2 * z + 1 - core + (32 - 2 * s if way == 0 else 2 * s), 16)

    for s in range(1, 5):
        for h in range(H):
            for way in range(2):
                piece = group(h, origin(way, s)) if s < 4 else group(h, origin(way, s), 4 * way, 4)
                copies.arrived(("gz", h, way, s), piece, z_next[way])
                if s < 3:
                    copies.send(("gz", h, way, s + 1), piece, piece, z_next[way])
                elif s == 3:
                    half = group(h, origin(way, s), 4 * way, 4)
                    copies.send(("gz", h, way, 4), half, half, z_next[way])
                copies.send(("gs", h, way, s), piece, piece, sibling)
    for h in range(H):
        copies.arrived(("gs", h, 0, 0), group(h, 2 * z + 1 - core), sibling)
        for s in range(1, 5):
            for way in range(2):
                number = origin_sibling(way, s)
                piece = group(h, number) if s < 4 else group(h, number, 4 * way, 4)
                copies.arrived(("gs", h, way, s), piece, sibling)
    load_values.wait()

    def product(side, panel, out):
        contract = (((1,), (1,)), ((), ())) if side == 0 else (((1,), (0,)), ((), ()))

        def some_slots(step, total):
            for u in range(UNROLL):
                k = step * UNROLL + u
                code = codes[side * slots + k]
                block = values[code & 511]
                piece = panel[:, code >> 9].reshape(128, 128)
                term = lax.dot_general(piece, block, contract, preferred_element_type=F32)
                total = total * keeps[side * slots + k] + term
                sums[k] = total.astype(BF16)
            return total

        lax.fori_loop(0, slots // UNROLL, some_slots, jnp.zeros((128, 128), F32))

        def some_blocks(step, carry):
            for u in range(8):
                q = step * 8 + u
                out[:, q] = sums[lasts[side * 128 + q]].reshape(H, PH, 128)
            return carry

        lax.fori_loop(0, 16, some_blocks, 0)

    product(0, gathered, partial)

    def slab(h, path, d1, first=0, count=4):
        return (h, pl.ds(path * 64 + d1 * 16 + first * 4, count * 4))

    for h, path in chunks:
        axis = axes[path][0]
        m = position[axis]
        for way in range(2):
            far = lax.rem(m + 2, 4)
            near = lax.rem(m + (1 if way == 0 else 3), 4)
            src = partial.at[slab(h, path, far, 2 * way, 2)]
            copies.send(("r1", h, path, way, 0), src, relay1.at[h, path, way], nearby[axis][way])
            src = partial.at[slab(h, path, near, 2 - 2 * way, 2)]
            dst = full1.at[h, path, way, pl.ds(8 - 8 * way, 8)]
            copies.send(("r1", h, path, way, 1), src, dst, nearby[axis][way])
    for h, path in chunks:
        axis = axes[path][0]
        m = position[axis]
        for way in range(2):
            near = lax.rem(m + (1 if way == 0 else 3), 4)
            copies.arrived(("r1", h, path, way, 0), relay1.at[h, path, way], nearby[axis][way])
            where = slab(h, path, near, 2 * way, 2)
            partial[where] = (partial[where].astype(F32) + relay1[h, path, way].astype(F32)).astype(BF16)
            dst = full1.at[h, path, way, pl.ds(8 * way, 8)]
            copies.send(("r1", h, path, way, 2), partial.at[where], dst, nearby[axis][way])
    for h, path in chunks:
        axis, other = axes[path]
        m, m2 = position[axis], position[other]
        for way in range(2):
            copies.arrived(
                ("r1", h, path, way, 1), full1.at[h, path, way, pl.ds(8 - 8 * way, 8)], nearby[axis][way]
            )
            copies.arrived(("r1", h, path, way, 2), full1.at[h, path, way, pl.ds(8 * way, 8)], nearby[axis][way])
        for d2 in range(4):
            total = partial[slab(h, path, m, d2, 1)].astype(F32)
            for way in range(2):
                total = total + full1[h, path, way, 4 * d2 : 4 * d2 + 4].astype(F32)
            mid_own[h, path, d2] = total
            mid[h, path, d2] = total.astype(BF16)
        for way in range(2):
            far = lax.rem(m2 + 2, 4)
            near = lax.rem(m2 + (1 if way == 0 else 3), 4)
            src = mid.at[h, path, far, pl.ds(2 * way, 2)]
            copies.send(("r2", h, path, way, 0), src, relay2.at[h, path, way], nearby[other][way])
            src = mid.at[h, path, near, pl.ds(2 - 2 * way, 2)]
            dst = full2.at[h, path, way, pl.ds(2 - 2 * way, 2)]
            copies.send(("r2", h, path, way, 1), src, dst, nearby[other][way])
    for h, path in chunks:
        other = axes[path][1]
        m2 = position[other]
        for way in range(2):
            near = lax.rem(m2 + (1 if way == 0 else 3), 4)
            copies.arrived(("r2", h, path, way, 0), relay2.at[h, path, way], nearby[other][way])
            where = (h, path, near, pl.ds(2 * way, 2))
            mid[where] = (mid_own[where] + relay2[h, path, way].astype(F32)).astype(BF16)
            dst = full2.at[h, path, way, pl.ds(2 * way, 2)]
            copies.send(("r2", h, path, way, 2), mid.at[where], dst, nearby[other][way])

    def piece(h, path, d1, d2, first=0, count=4):
        return left_all.at[h, pl.ds(path * 64 + d1 * 16 + d2 * 4 + first, count)]

    for h, path in chunks:
        axis, other = axes[path]
        m1, m2 = position[axis], position[other]
        for way in range(2):
            copies.arrived(("r2", h, path, way, 1), full2.at[h, path, way, pl.ds(2 - 2 * way, 2)], nearby[other][way])
            copies.arrived(("r2", h, path, way, 2), full2.at[h, path, way, pl.ds(2 * way, 2)], nearby[other][way])
        total = mid_own[h, path, m2]
        for way in range(2):
            total = total + full2[h, path, way].astype(F32)
        rounded = total.astype(BF16)
        left_all[h, pl.ds(path * 64 + m1 * 16 + m2 * 4, 4)] = rounded
        for b in range(4):
            left_y[path * 4 + b, PH * h : PH * h + PH, :] = rounded[b]
        own = piece(h, path, m1, m2)
        for way in range(2):
            copies.send(("a2", h, path, 0, way, 0), own, own, nearby[axis][way])
        for way in range(2):
            copies.send(("a1", h, path, way, 0), own, own, nearby[other][way])

    def gram_begin(tag, blocks):
        total = jnp.zeros((128, 128), F32)
        for b in range(8):
            part = blocks[b]
            total = total + lax.dot_general(part, part, (((1,), (1,)), ((), ())), preferred_element_type=F32)
        gram_part[tag] = total * (1.0 / nodes_total)
        gram_in1[tag, r] = gram_part[tag, pl.ds(pl.multiple_of(r * 8, 8), 8), :]
        for t in range(1, 16):
            to = lax.rem(r + t, 16)
            src = gram_part.at[tag, pl.ds(pl.multiple_of(to * 8, 8), 8), :]
            copies.send(("m1", tag, t), src, gram_in1.at[tag, r], {"row": to})

    def gram_middle(tag):
        for t in range(1, 16):
            copies.arrived(("m1", tag, t), gram_in1.at[tag, lax.rem(r + 16 - t, 16)], {"row": lax.rem(r + t, 16)})
        gram_slice[tag] = jnp.sum(gram_in1[tag], axis=0)
        gram_in2[tag, c] = gram_slice[tag]
        for t in range(1, 16):
            copies.send(("m2", tag, t), gram_slice.at[tag], gram_in2.at[tag, c], {"col": lax.rem(c + t, 16)})

    def gram_last(tag):
        for t in range(1, 16):
            copies.arrived(("m2", tag, t), gram_in2.at[tag, lax.rem(c + 16 - t, 16)], {"col": lax.rem(c + t, 16)})
        mine = gram_total.at[tag, pl.ds(pl.multiple_of(r * 8, 8), 8), :]
        mine[...] = jnp.sum(gram_in2[tag], axis=0)
        for t in range(1, 16):
            copies.send(("m3", tag, t), mine, mine, {"row": lax.rem(r + t, 16)})

    def gram_end(tag):
        for t in range(1, 16):
            rows = pl.ds(pl.multiple_of(lax.rem(r + 16 - t, 16) * 8, 8), 8)
            copies.arrived(("m3", tag, t), gram_total.at[tag, rows, :], {"row": lax.rem(r + t, 16)})

    gram_begin(0, left_y)
    for h, path in chunks:
        axis, other = axes[path]
        m1, m2 = position[axis], position[other]
        for way in range(2):
            d2 = lax.rem(m2 + (3 if way == 0 else 1), 4)
            copies.arrived(("a1", h, path, way, 0), piece(h, path, m1, d2), nearby[other][way])
            half = piece(h, path, m1, d2, 2 * way, 2)
            copies.send(("a1", h, path, way, 1), half, half, nearby[other][way])
            whole = piece(h, path, m1, d2)
            for way2 in range(2):
                copies.send(("a2", h, path, 1 + way, way2, 0), whole, whole, nearby[axis][way2])
    gram_middle(0)
    for h, path in chunks:
        axis, other = axes[path]
        m1, m2 = position[axis], position[other]
        far = lax.rem(m2 + 2, 4)
        for way in range(2):
            copies.arrived(("a1", h, path, way, 1), piece(h, path, m1, far, 2 * way, 2), nearby[other][way])
        whole = piece(h, path, m1, far)
        for way2 in range(2):
            copies.send(("a2", h, path, 3, way2, 0), whole, whole, nearby[axis][way2])
    gram_last(0)

    def second(m2, which):
        return lax.rem(m2 + (0, 3, 1, 2)[which], 4)

    for which in range(4):
        for h, path in chunks:
            axis, other = axes[path]
            m1, m2 = position[axis], position[other]
            d2 = second(m2, which)
            for way in range(2):
                d1 = lax.rem(m1 + (3 if way == 0 else 1), 4)
                copies.arrived(("a2", h, path, which, way, 0), piece(h, path, d1, d2), nearby[axis][way])
                half = piece(h, path, d1, d2, 2 * way, 2)
                copies.send(("a2", h, path, which, way, 1), half, half, nearby[axis][way])
        if which == 1:
            gram_end(0)
    factor_inverse(gram_total.at[0], work, inv1)
    for which in range(4):
        for h, path in chunks:
            axis, other = axes[path]
            far = lax.rem(position[axis] + 2, 4)
            d2 = second(position[other], which)
            for way in range(2):
                copies.arrived(
                    ("a2", h, path, which, way, 1), piece(h, path, far, d2, 2 * way, 2), nearby[axis][way]
                )

    product(1, left_all, partial2)

    def for_z(distance):
        return lax.rem(z + 8 + distance, 8)

    def theirs(h, which_core, distance):
        return partial2.at[h, pl.ds(which_core * 64 + for_z(distance) * 8, 8)]

    order = (4, 3, -3, 2, -2, 1, -1, 0)
    for distance in order:
        for h in range(H):
            copies.send(
                ("ps", h, distance), theirs(h, 1 - core, distance), pair_in.at[h, distance + 3], sibling
            )

    def pair_sum(h, distance):
        copies.arrived(("ps", h, distance), pair_in.at[h, distance + 3], sibling)
        mine = partial2[h, pl.ds(core * 64 + for_z(distance) * 8, 8)]
        return mine.astype(F32) + pair_in[h, distance + 3].astype(F32)

    for h in range(H):
        rounded = pair_sum(h, 4).astype(BF16)
        for way in range(2):
            ring_out[h, way, 0, 0:4] = rounded[4 * way : 4 * way + 4]
            copies.send(
                ("rz", h, way, 0),
                ring_out.at[h, way, 0, pl.ds(0, 4)],
                ring_in.at[h, way, 0, pl.ds(0, 4)],
                z_next[way],
            )
    for s in range(1, 4):
        for h in range(H):
            for way in range(2):
                total = pair_sum(h, (4 - s) if way == 0 else (s - 4))
                if s == 1:
                    came = ring_in.at[h, way, 0, pl.ds(0, 4)]
                    copies.arrived(("rz", h, way, 0), came, z_next[way])
                    added = total[4 * way : 4 * way + 4] + came[...].astype(F32)
                    kept = total[4 - 4 * way : 8 - 4 * way]
                    ring_out[h, way, s, 4 * way : 4 * way + 4] = added.astype(BF16)
                    ring_out[h, way, s, 4 - 4 * way : 8 - 4 * way] = kept.astype(BF16)
                else:
                    came = ring_in.at[h, way, s - 1]
                    copies.arrived(("rz", h, way, s - 1), came, z_next[way])
                    ring_out[h, way, s] = (total + came[...].astype(F32)).astype(BF16)
                copies.send(("rz", h, way, s), ring_out.at[h, way, s], ring_in.at[h, way, s], z_next[way])

    def apply(inverse, block):
        return jnp.dot(inverse, block, precision=HIGHEST, preferred_element_type=F32)

    for b in range(8):
        left_out[128 * b : 128 * b + 128, :] = apply(inv1[...], left_y[b].astype(F32)).T.astype(BF16)

    for h in range(H):
        total = pair_sum(h, 0)
        for way in range(2):
            copies.arrived(("rz", h, way, 3), ring_in.at[h, way, 3], z_next[way])
            total = total + ring_in[h, way, 3].astype(F32)
        for b in range(8):
            z_sum[b, PH * h : PH * h + PH, :] = total[b]
    for b in range(8):
        right_y[b] = apply(inv1[...], z_sum[b]).astype(BF16)
    gram_begin(1, right_y)
    gram_middle(1)
    gram_last(1)
    gram_end(1)
    factor_inverse(gram_total.at[1], work, inv2)
    for b in range(8):
        right_out[128 * b : 128 * b + 128, :] = apply(inv2[...], right_y[b].astype(F32)).T.astype(BF16)
    copies.drain()


def slot_order(rows, cols, count):
    slots = rows.shape[0]
    number = jnp.arange(slots, dtype=jnp.int32)
    live = number < count
    group, b = rows // 8, rows % 8
    gx, gy = group // 4, group % 4
    path, blk = b // 4, b % 4
    row_place = path * 64 + jnp.where(path == 0, gx * 16 + gy * 4, gy * 16 + gx * 4) + blk
    key = jnp.where(live[None, :], jnp.stack([rows, cols]), 128)
    inputs = jnp.stack([cols, row_place])
    packed = number[None, :] + 512 * inputs + 65536 * key
    ahead = (key[:, None, :] < key[:, :, None]) | (
        (key[:, None, :] == key[:, :, None]) & (number[None, None, :] < number[None, :, None])
    )
    rank = jnp.sum(ahead.astype(jnp.int32), axis=2)
    hit = rank[:, :, None] == number[None, None, :]
    in_order = jnp.sum(jnp.where(hit, packed[:, :, None], 0), axis=1)
    codes = in_order & 65535
    key_order = in_order >> 16
    keeps = jnp.concatenate(
        [jnp.zeros((2, 1), F32), (key_order[:, 1:] == key_order[:, :-1]).astype(F32)], axis=1
    )
    q = jnp.arange(128, dtype=jnp.int32)
    path, d1, d2, blk = q // 64, q // 16 % 4, q // 4 % 4, q % 4
    left_block = jnp.where(path == 0, d1 * 4 + d2, d2 * 4 + d1) * 8 + path * 4 + blk
    right_block = (2 * (q // 8 % 8) + q // 64) * 8 + q % 8
    block = jnp.stack([left_block, right_block])
    upto = jnp.sum((key[:, :, None] <= block[:, None, :]).astype(jnp.int32), axis=1)
    below = jnp.sum((key[:, :, None] < block[:, None, :]).astype(jnp.int32), axis=1)
    lasts = jnp.where(upto > below, upto - 1, slots)
    return codes.reshape(-1), keeps.reshape(-1), lasts.reshape(-1)


def local(start_panel, block_values, block_rows, block_cols, block_counts):
    slots = block_values.shape[2]
    group_rows, width = start_panel.shape
    nodes_total = group_rows * lax.axis_size("row") * lax.axis_size("col")
    codes, keeps, lasts = slot_order(block_rows[0, 0], block_cols[0, 0], block_counts[0, 0])
    vmem = pl.BlockSpec(memory_space=pltpu.VMEM)
    smem = pl.BlockSpec(memory_space=pltpu.SMEM)
    panel = jax.ShapeDtypeStruct((group_rows, width), BF16)
    tile = pltpu.VMEM((H, 128, PH, 128), BF16)
    return pl.pallas_call(
        functools.partial(kernel, nodes_total),
        out_shape=(panel, panel),
        in_specs=[smem, smem, smem, vmem, pl.BlockSpec(memory_space=pl.ANY)],
        out_specs=(vmem, vmem),
        scratch_shapes=[
            pltpu.VMEM((slots, 128, 128), BF16),
            tile,
            pltpu.VMEM((slots + 1, 128, 128), BF16),
            tile,
            tile,
            pltpu.VMEM((H, 2, 2, 8, PH, 128), BF16),
            pltpu.VMEM((H, 2, 2, 16, PH, 128), BF16),
            pltpu.VMEM((H, 2, 4, 4, PH, 128), BF16),
            pltpu.VMEM((H, 2, 4, 4, PH, 128), F32),
            pltpu.VMEM((H, 2, 2, 2, PH, 128), BF16),
            pltpu.VMEM((H, 2, 2, 4, PH, 128), BF16),
            tile,
            pltpu.VMEM((8, 128, 128), BF16),
            pltpu.VMEM((H, 8, 8, PH, 128), BF16),
            pltpu.VMEM((H, 2, 4, 8, PH, 128), BF16),
            pltpu.VMEM((H, 2, 4, 8, PH, 128), BF16),
            pltpu.VMEM((8, 128, 128), F32),
            pltpu.VMEM((8, 128, 128), BF16),
            pltpu.VMEM((2, 128, 128), F32),
            pltpu.VMEM((2, 16, 8, 128), F32),
            pltpu.VMEM((2, 8, 128), F32),
            pltpu.VMEM((2, 16, 8, 128), F32),
            pltpu.VMEM((2, 128, 128), F32),
            pltpu.VMEM((128, 128), F32),
            pltpu.VMEM((128, 128), F32),
            pltpu.VMEM((128, 128), F32),
            pltpu.SemaphoreType.DMA,
            pltpu.SemaphoreType.DMA((SENDS,)),
            pltpu.SemaphoreType.DMA((SENDS,)),
        ],
        compiler_params=pltpu.CompilerParams(
            collective_id=0, has_side_effects=True, vmem_limit_bytes=60 * 2**20
        ),
        cost_estimate=pl.CostEstimate(
            flops=4 * slots * 128**3, bytes_accessed=2 * slots * 128 * 128, transcendentals=0
        ),
    )(codes, keeps, lasts, start_panel, block_values[0, 0])


def solution(mesh):
    return jax.shard_map(
        local,
        mesh=mesh,
        in_specs=(
            P(("col", "row"), None),
            P("row", "col", None, None, None),
            P("row", "col", None),
            P("row", "col", None),
            P("row", "col"),
        ),
        out_specs=(P(("row", "col"), None), P(("col", "row"), None)),
        check_vma=False,
    )
```

```python
import functools

import jax
import jax.numpy as jnp
from jax import lax
from jax.experimental import pallas as pl
from jax.experimental.pallas import tpu as pltpu
from jax.sharding import PartitionSpec as P

MESH = pl.DeviceIdType.MESH
F32 = jnp.float32
BF16 = jnp.bfloat16
HIGHEST = lax.Precision.HIGHEST

H = 2
PH = 64
NZ = 8
UNROLL = 16
PARTS = 4
SENDS = 440
GATHER_CUTS = 4
COLUMN_CUTS = 2


class Copies:
    def __init__(self, send_sems, recv_sems):
        self.send_sems, self.recv_sems = send_sems, recv_sems
        self.index, self.sent = {}, []

    def sems(self, name):
        number = self.index.setdefault(name, len(self.index))
        assert number < SENDS
        return self.send_sems.at[number], self.recv_sems.at[number]

    def make(self, name, src, dst, device):
        send, recv = self.sems(name)
        return pltpu.make_async_remote_copy(
            src_ref=src, dst_ref=dst, send_sem=send, recv_sem=recv, device_id=device, device_id_type=MESH
        )

    def send(self, name, src, dst, device):
        copy = self.make(name, src, dst, device)
        copy.start()
        self.sent.append(copy)

    def arrived(self, name, dst, device):
        self.make(name, dst, dst, device).wait_recv()

    def drain(self):
        for copy in self.sent:
            copy.wait_send()
        self.sent = []


def split3(value):
    high = value.astype(BF16).astype(F32)
    rest = value - high
    middle = rest.astype(BF16).astype(F32)
    return high, middle, (rest - middle).astype(BF16).astype(F32)


def factor_begin(gram, work):
    n = gram.shape[0]
    rows = lax.broadcasted_iota(jnp.int32, (n, n), 0)
    cols = lax.broadcasted_iota(jnp.int32, (n, n), 1)
    work[:, :n] = gram
    work[:, n:] = jnp.where(rows == cols, 1.0, 0.0).astype(F32)


def factor_blocks(work, first, last):
    n = work.shape[0]
    lanes = lax.broadcasted_iota(jnp.int32, (16, n), 1)
    subs = lax.broadcasted_iota(jnp.int32, (8, n), 0)

    def block(jb, carry):
        start = pl.multiple_of(jb * 16, 16)
        rows = work[pl.ds(start, 16), :]
        turned = pltpu.roll(rows[:, :n], lax.rem(n - start, n), 1)
        top = [jnp.broadcast_to(turned[:8, i : i + 1], (8, n)) for i in range(16)]
        low = [jnp.broadcast_to(turned[8:, i : i + 1], (8, n)) for i in range(16)]
        rows_top = [rows[:8, :n], rows[:8, n:]]
        rows_low = [rows[8:, :n], rows[8:, n:]]
        scales = [jnp.zeros((8, n), F32), jnp.zeros((8, n), F32)]
        for i in range(16):
            half, sub = i // 8, i % 8
            source, source_rows = (top, rows_top) if half == 0 else (low, rows_low)
            inverse = jnp.broadcast_to(1.0 / source[i][sub : sub + 1, :], (8, n))
            scales[half] = jnp.where(subs == sub, inverse, scales[half])
            pivots = {j: source[j][sub : sub + 1, :] for j in range(i + 1, 16)}
            pivot_rows = [value[sub : sub + 1, :] for value in source_rows]
            if half == 0:
                factor = jnp.where(subs > sub, top[i] * inverse, 0.0)
                for j in range(i + 1, 16):
                    top[j] = top[j] - factor * pivots[j]
                rows_top = [value - factor * pivot for value, pivot in zip(rows_top, pivot_rows)]
                factor = low[i] * inverse
            else:
                factor = jnp.where(subs > sub, low[i] * inverse, 0.0)
            for j in range(i + 1, 16):
                low[j] = low[j] - factor * pivots[j]
            rows_low = [value - factor * pivot for value, pivot in zip(rows_low, pivot_rows)]
        scale = jnp.concatenate(scales, axis=0)
        d = jnp.concatenate([rows_top[0], rows_low[0]], axis=0)
        m = jnp.concatenate([rows_top[1], rows_low[1]], axis=0)
        left = split3(jnp.where(lanes >= start + 16, d * scale, 0.0))
        right = split3(jnp.concatenate([d, m], axis=1))
        pairs = ((0, 0), (0, 1), (1, 0), (1, 1), (0, 2), (2, 0))
        stacked_left = jnp.concatenate([left[a] for a, _ in pairs], axis=0).T.astype(BF16)
        stacked_right = jnp.concatenate([right[b] for _, b in pairs], axis=0).astype(BF16)
        work[...] = work[...] - jnp.dot(stacked_left, stacked_right, preferred_element_type=F32)
        work[pl.ds(start, 16), n:] = m * jnp.sqrt(scale)
        return carry

    lax.fori_loop(first, last, block, 0)


def kernel(
    nodes_total,
    codes,
    keeps,
    lasts,
    start_ref,
    values_hbm,
    left_y,
    right_y,
    inv1,
    inv2,
    values,
    gathered0,
    gathered1,
    sums,
    run_total,
    partial,
    partial2,
    relay1,
    full1,
    mid,
    mid_own,
    full2,
    left_all0,
    left_all1,
    pair_in,
    ring_out,
    ring_in,
    near_sum,
    z_sum,
    gram_part,
    gram_in1,
    gram_slice,
    gram_in2,
    gram_total,
    work,
    local_sem,
    send_sems,
    recv_sems,
):
    gathered, left_all = (gathered0, gathered1), (left_all0, left_all1)
    slots = values_hbm.shape[0]
    r = lax.axis_index("row")
    c = lax.axis_index("col")
    z, core = r // 2, lax.rem(r, 2)
    position = {"x": c // 4, "y": lax.rem(c, 4)}
    x, y = position["x"], position["y"]
    sibling = {"row": 2 * z + 1 - core}
    z_next = ({"row": lax.rem(r + 2, 16)}, {"row": lax.rem(r + 14, 16)})
    nearby = {
        "x": ({"col": lax.rem(c + 4, 16)}, {"col": lax.rem(c + 12, 16)}),
        "y": ({"col": 4 * x + lax.rem(y + 1, 4)}, {"col": 4 * x + lax.rem(y + 3, 4)}),
    }
    along = {
        "x": [{"col": lax.rem(c + 4 * e, 16)} for e in range(4)],
        "y": [{"col": 4 * x + lax.rem(y + e, 4)} for e in range(4)],
    }
    axes = (("x", "y"), ("y", "x"))
    copies = Copies(send_sems, recv_sems)
    paths = range(2)

    load_values = pltpu.make_async_copy(values_hbm, values, local_sem)
    load_values.start()

    barrier = pltpu.get_barrier_semaphore()
    for t in range(1, 16):
        pl.semaphore_signal(barrier, inc=1, device_id={"row": lax.rem(r + t, 16)}, device_id_type=MESH)
        pl.semaphore_signal(barrier, inc=1, device_id={"col": lax.rem(c + t, 16)}, device_id_type=MESH)

    for b in range(8):
        turned = start_ref[128 * b : 128 * b + 128, :].astype(F32).T.astype(BF16)
        for h in range(H):
            gathered[h][r * 8 + b] = turned[PH * h : PH * h + PH, :]
    sums[slots] = jnp.zeros((PH, 128), BF16)
    pl.semaphore_wait(barrier, 30)

    def group(h, number, first=0, count=8):
        return gathered[h].at[pl.ds(number * 8 + first, count)]

    def origin(way, s):
        return lax.rem(r + (32 - 2 * s if way == 0 else 2 * s), 16)

    def origin_sibling(way, s):
        return lax.rem(2 * z + 1 - core + (32 - 2 * s if way == 0 else 2 * s), 16)

    cut = 8 // GATHER_CUTS

    def gather_begin(h):
        for q in range(GATHER_CUTS):
            own = group(h, r, cut * q, cut)
            for way in range(2):
                copies.send(("gz", h, way, 1, q), own, own, z_next[way])
        own = group(h, r)
        copies.send(("gs", h, 0, 0), own, own, sibling)

    def last_cuts(way):
        return range(way * GATHER_CUTS // 2, (way + 1) * GATHER_CUTS // 2)

    def gather_step(h, s):
        for q in range(GATHER_CUTS):
            for way in range(2):
                if s == 4 and q not in last_cuts(way):
                    continue
                part = group(h, origin(way, s), cut * q, cut)
                copies.arrived(("gz", h, way, s, q), part, z_next[way])
                if s < 3 or (s == 3 and q in last_cuts(way)):
                    copies.send(("gz", h, way, s + 1, q), part, part, z_next[way])
        for way in range(2):
            whole = group(h, origin(way, s)) if s < 4 else group(h, origin(way, s), 4 * way, 4)
            copies.send(("gs", h, way, s), whole, whole, sibling)

    def gather_end(h):
        copies.arrived(("gs", h, 0, 0), group(h, 2 * z + 1 - core), sibling)
        for s in range(1, 5):
            for way in range(2):
                number = origin_sibling(way, s)
                piece = group(h, number) if s < 4 else group(h, number, 4 * way, 4)
                copies.arrived(("gs", h, way, s), piece, sibling)

    def product(side, h, part):
        contract = (((1,), (1,)), ((), ())) if side == 0 else (((1,), (0,)), ((), ()))
        panel = gathered[h] if side == 0 else left_all[h]
        steps = slots // UNROLL

        def some_slots(step, total):
            for u in range(UNROLL):
                k = step * UNROLL + u
                code = codes[side * slots + k]
                term = lax.dot_general(panel[code >> 9], values[code & 511], contract, preferred_element_type=F32)
                total = total * keeps[side * slots + k] + term
                sums[k] = total.astype(BF16)
            return total

        total = jnp.zeros((PH, 128), F32) if part == 0 else run_total[...]
        run_total[...] = lax.fori_loop(steps * part // PARTS, steps * (part + 1) // PARTS, some_slots, total)

    def place(side, h):
        out = partial if side == 0 else partial2

        def some_blocks(step, carry):
            for u in range(8):
                q = step * 8 + u
                out[h, q] = sums[lasts[side * 128 + q]]
            return carry

        lax.fori_loop(0, 16, some_blocks, 0)

    def slab(h, path, d1, first=0, count=4):
        return (h, pl.ds(path * 64 + d1 * 16 + first * 4, count * 4))

    def reduce1(h):
        for n in range(2):
            for path in paths:
                axis = axes[path][0]
                far = lax.rem(position[axis] + 2, 4)
                for way in range(2):
                    src = partial.at[slab(h, path, far, 2 * way + n, 1)]
                    dst = relay1.at[h, path, way, pl.ds(4 * n, 4)]
                    copies.send(("r1", h, path, way, n), src, dst, nearby[axis][way])
        for path in paths:
            axis = axes[path][0]
            for way in range(2):
                near = lax.rem(position[axis] + (1 if way == 0 else 3), 4)
                src = partial.at[slab(h, path, near, 2 - 2 * way, 2)]
                dst = full1.at[h, path, way, pl.ds(8 - 8 * way, 8)]
                copies.send(("r1", h, path, way, 2), src, dst, nearby[axis][way])

    def reduce2(h):
        for n in range(2):
            for path in paths:
                axis = axes[path][0]
                for way in range(2):
                    near = lax.rem(position[axis] + (1 if way == 0 else 3), 4)
                    came = relay1.at[h, path, way, pl.ds(4 * n, 4)]
                    copies.arrived(("r1", h, path, way, n), came, nearby[axis][way])
                    where = slab(h, path, near, 2 * way + n, 1)
                    partial[where] = (partial[where].astype(F32) + came[...].astype(F32)).astype(BF16)
                    dst = full1.at[h, path, way, pl.ds(8 * way + 4 * n, 4)]
                    copies.send(("r1", h, path, way, 3 + n), partial.at[where], dst, nearby[axis][way])

    def reduce3(h):
        for path in paths:
            axis, other = axes[path]
            m, m2 = position[axis], position[other]
            for way in range(2):
                came = full1.at[h, path, way]
                copies.arrived(("r1", h, path, way, 2), came.at[pl.ds(8 - 8 * way, 8)], nearby[axis][way])
                for n in range(2):
                    copies.arrived(
                        ("r1", h, path, way, 3 + n), came.at[pl.ds(8 * way + 4 * n, 4)], nearby[axis][way]
                    )
            for e in (2, 1, 3, 0):
                d2 = lax.rem(m2 + e, 4)
                total = partial[slab(h, path, m, d2, 1)].astype(F32)
                for way in range(2):
                    total = total + full1[h, path, way, pl.ds(4 * d2, 4)].astype(F32)
                if e == 0:
                    mid_own[h, path] = total
                else:
                    mid[h, path, e - 1] = total.astype(BF16)
                    copies.send(
                        ("r2", h, path, e), mid.at[h, path, e - 1], full2.at[h, path, e - 1], along[other][e]
                    )

    def piece(h, path, d1, d2, first=0, count=4):
        return left_all[h].at[pl.ds(path * 64 + d1 * 16 + d2 * 4 + first, count)]

    def reduce4(h):
        for path in paths:
            axis, other = axes[path]
            m1, m2 = position[axis], position[other]
            total = mid_own[h, path]
            for e in (1, 3, 2):
                copies.arrived(("r2", h, path, e), full2.at[h, path, e - 1], along[other][e])
                total = total + full2[h, path, e - 1].astype(F32)
            rounded = total.astype(BF16)
            left_all[h][pl.ds(path * 64 + m1 * 16 + m2 * 4, 4)] = rounded
            for b in range(4):
                at = 128 * (path * 4 + b)
                left_y[PH * h : PH * h + PH, at : at + 128] = rounded[b]
            own = piece(h, path, m1, m2)
            for e in (2, 1, 3):
                copies.send(("a1", h, path, e), own, own, along[other][e])
            for way in range(2):
                copies.send(("a2", h, path, 0, way, 0), own, own, nearby[axis][way])

    def gram_begin(tag, panel):
        total = lax.dot_general(panel, panel, (((1,), (1,)), ((), ())), preferred_element_type=F32)
        gram_part[tag] = total * (1.0 / nodes_total)
        gram_in1[tag, r] = gram_part[tag, pl.ds(pl.multiple_of(r * 8, 8), 8), :]
        for t in range(1, 16):
            to = lax.rem(r + t, 16)
            src = gram_part.at[tag, pl.ds(pl.multiple_of(to * 8, 8), 8), :]
            copies.send(("m1", tag, t), src, gram_in1.at[tag, r], {"row": to})

    def gram_middle(tag):
        for t in range(1, 16):
            copies.arrived(("m1", tag, t), gram_in1.at[tag, lax.rem(r + 16 - t, 16)], {"row": lax.rem(r + t, 16)})
        gram_slice[tag] = jnp.sum(gram_in1[tag], axis=0)
        gram_in2[tag, c] = gram_slice[tag]
        for t in range(1, 16):
            copies.send(("m2", tag, t), gram_slice.at[tag], gram_in2.at[tag, c], {"col": lax.rem(c + t, 16)})

    def gram_last(tag):
        for t in range(1, 16):
            copies.arrived(("m2", tag, t), gram_in2.at[tag, lax.rem(c + 16 - t, 16)], {"col": lax.rem(c + t, 16)})
        mine = gram_total.at[tag, pl.ds(pl.multiple_of(r * 8, 8), 8), :]
        mine[...] = jnp.sum(gram_in2[tag], axis=0)
        for t in range(1, 16):
            copies.send(("m3", tag, t), mine, mine, {"row": lax.rem(r + t, 16)})

    def gram_end(tag):
        for t in range(1, 16):
            rows = pl.ds(pl.multiple_of(lax.rem(r + 16 - t, 16) * 8, 8), 8)
            copies.arrived(("m3", tag, t), gram_total.at[tag, rows, :], {"row": lax.rem(r + t, 16)})

    def second(m2, e):
        return lax.rem(m2 + 4 - e, 4)

    def spread1(h):
        for e in (1, 3, 2):
            for path in paths:
                axis, other = axes[path]
                whole = piece(h, path, position[axis], second(position[other], e))
                copies.arrived(("a1", h, path, e), whole, along[other][e])
                for way in range(2):
                    copies.send(("a2", h, path, e, way, 0), whole, whole, nearby[axis][way])

    def spread3(h, which):
        for path in paths:
            axis, other = axes[path]
            m1, m2 = position[axis], position[other]
            d2 = second(m2, which)
            for way in range(2):
                d1 = lax.rem(m1 + (3 if way == 0 else 1), 4)
                copies.arrived(("a2", h, path, which, way, 0), piece(h, path, d1, d2), nearby[axis][way])
                half = piece(h, path, d1, d2, 2 * way, 2)
                copies.send(("a2", h, path, which, way, 1), half, half, nearby[axis][way])

    def spread_end(h):
        for which in (0, 1, 3, 2):
            for path in paths:
                axis, other = axes[path]
                far = lax.rem(position[axis] + 2, 4)
                d2 = second(position[other], which)
                for way in range(2):
                    copies.arrived(
                        ("a2", h, path, which, way, 1), piece(h, path, far, d2, 2 * way, 2), nearby[axis][way]
                    )

    def for_z(distance):
        return lax.rem(z + 8 + distance, 8)

    def column0(h):
        for distance in (4, 3, -3, 2, -2, 1, -1, 0):
            src = partial2.at[h, pl.ds((1 - core) * 64 + for_z(distance) * 8, 8)]
            copies.send(("ps", h, distance), src, pair_in.at[h, distance + 3], sibling)

    def pair_sum(h, distance):
        copies.arrived(("ps", h, distance), pair_in.at[h, distance + 3], sibling)
        mine = partial2[h, pl.ds(core * 64 + for_z(distance) * 8, 8)]
        return mine.astype(F32) + pair_in[h, distance + 3].astype(F32)

    span = 8 // COLUMN_CUTS

    def far_cut(way, q):
        return q // (COLUMN_CUTS // 2) == way

    def column_send(h, way, s, q, total):
        at = pl.ds(span * q, span)
        ring_out[h, way, s, at] = total.astype(BF16)
        copies.send(
            ("rz", h, way, s, q), ring_out.at[h, way, s, at], ring_in.at[h, way, s, at], z_next[way]
        )

    def column1(h):
        total = pair_sum(h, 4)
        for q in range(COLUMN_CUTS):
            for way in range(2):
                if far_cut(way, q):
                    column_send(h, way, 0, q, total[span * q : span * q + span])
        for way in range(2):
            total = pair_sum(h, 3 - 6 * way)
            near_sum[h, way] = total
            for q in range(COLUMN_CUTS):
                if not far_cut(way, q):
                    column_send(h, way, 1, q, total[span * q : span * q + span])

    def column2(h, s):
        if s > 1:
            for way in range(2):
                near_sum[h, way] = pair_sum(h, (4 - s) * (1 - 2 * way))
        for first in (True, False):
            for q in range(COLUMN_CUTS):
                for way in range(2):
                    far = far_cut(way, q)
                    if far == first or (s == 1 and not far):
                        continue
                    at = pl.ds(span * q, span)
                    came = ring_in.at[h, way, s - 1, at]
                    copies.arrived(("rz", h, way, s - 1, q), came, z_next[way])
                    column_send(h, way, s, q, near_sum[h, way, at] + came[...].astype(F32))

    def column3(h):
        total = pair_sum(h, 0)
        for way in range(2):
            for q in range(COLUMN_CUTS):
                came = ring_in.at[h, way, 3, pl.ds(span * q, span)]
                copies.arrived(("rz", h, way, 3, q), came, z_next[way])
            total = total + ring_in[h, way, 3].astype(F32)
        for b in range(8):
            z_sum[PH * h : PH * h + PH, 128 * b : 128 * b + 128] = total[b]

    gather_begin(0)
    gather_step(0, 1)
    gather_begin(1)
    for s in (2, 3):
        gather_step(0, s)
        gather_step(1, s - 1)
    gather_step(0, 4)
    gather_end(0)
    load_values.wait()
    product(0, 0, 0)
    gather_step(1, 3)
    product(0, 0, 1)
    product(0, 0, 2)
    gather_step(1, 4)
    product(0, 0, 3)
    place(0, 0)
    reduce1(0)
    gather_end(1)
    product(0, 1, 0)
    product(0, 1, 1)
    reduce2(0)
    product(0, 1, 2)
    product(0, 1, 3)
    place(0, 1)
    reduce1(1)
    reduce3(0)
    reduce2(1)
    reduce4(0)
    reduce3(1)
    spread1(0)
    spread3(0, 0)
    reduce4(1)
    gram_begin(0, left_y[...])
    spread3(0, 1)
    spread3(0, 3)
    spread3(0, 2)
    spread1(1)
    spread_end(0)
    product(1, 0, 0)
    spread3(1, 0)
    product(1, 0, 1)
    spread3(1, 1)
    spread3(1, 3)
    product(1, 0, 2)
    spread3(1, 2)
    product(1, 0, 3)
    place(1, 0)
    column0(0)
    gram_middle(0)
    column1(0)
    spread_end(1)
    product(1, 1, 0)
    product(1, 1, 1)
    column2(0, 1)
    gram_last(0)
    product(1, 1, 2)
    product(1, 1, 3)
    place(1, 1)
    column0(1)
    column2(0, 2)
    column1(1)
    gram_end(0)
    factor_begin(gram_total[0], work)
    factor_blocks(work, 0, 2)
    column2(0, 3)
    column2(1, 1)
    factor_blocks(work, 2, 4)
    column3(0)
    column2(1, 2)
    factor_blocks(work, 4, 6)
    column2(1, 3)
    factor_blocks(work, 6, 8)
    inv1[...] = work[:, 128:]
    column3(1)
    right_sum = jnp.dot(inv1[...], z_sum[...], precision=HIGHEST, preferred_element_type=F32)
    right_y[...] = right_sum.astype(BF16)
    gram_begin(1, right_y[...])
    gram_middle(1)
    gram_last(1)
    gram_end(1)
    factor_begin(gram_total[1], work)
    factor_blocks(work, 0, 8)
    inv2[...] = work[:, 128:]
    copies.drain()


def apply_kernel(left_y, right_y, inv1, inv2, left_out, right_out):
    for y, inverse, out in ((left_y, inv1, left_out), (right_y, inv2, right_out)):
        parts = split3(inverse[...])
        total = sum(jnp.dot(part.astype(BF16), y[...], preferred_element_type=F32) for part in parts[::-1])
        for b in range(8):
            out[128 * b : 128 * b + 128, :] = total[:, 128 * b : 128 * b + 128].T.astype(BF16)


def slot_order(rows, cols, count):
    slots = rows.shape[0]
    number = jnp.arange(slots, dtype=jnp.int32)
    live = number < count
    group, b = rows // 8, rows % 8
    gx, gy = group // 4, group % 4
    path, blk = b // 4, b % 4
    row_place = path * 64 + jnp.where(path == 0, gx * 16 + gy * 4, gy * 16 + gx * 4) + blk
    key = jnp.where(live[None, :], jnp.stack([rows, cols]), 128)
    inputs = jnp.stack([cols, row_place])
    packed = number[None, :] + 512 * inputs + 65536 * key
    ahead = (key[:, None, :] < key[:, :, None]) | (
        (key[:, None, :] == key[:, :, None]) & (number[None, None, :] < number[None, :, None])
    )
    rank = jnp.sum(ahead.astype(jnp.int32), axis=2)
    hit = rank[:, :, None] == number[None, None, :]
    in_order = jnp.sum(jnp.where(hit, packed[:, :, None], 0), axis=1)
    codes = in_order & 65535
    key_order = in_order >> 16
    keeps = jnp.concatenate(
        [jnp.zeros((2, 1), F32), (key_order[:, 1:] == key_order[:, :-1]).astype(F32)], axis=1
    )
    q = jnp.arange(128, dtype=jnp.int32)
    path, d1, d2, blk = q // 64, q // 16 % 4, q // 4 % 4, q % 4
    left_block = jnp.where(path == 0, d1 * 4 + d2, d2 * 4 + d1) * 8 + path * 4 + blk
    right_block = (2 * (q // 8 % 8) + q // 64) * 8 + q % 8
    block = jnp.stack([left_block, right_block])
    upto = jnp.sum((key[:, :, None] <= block[:, None, :]).astype(jnp.int32), axis=1)
    below = jnp.sum((key[:, :, None] < block[:, None, :]).astype(jnp.int32), axis=1)
    lasts = jnp.where(upto > below, upto - 1, slots)
    return codes.reshape(-1), keeps.reshape(-1), lasts.reshape(-1)


def local(start_panel, block_values, block_rows, block_cols, block_counts):
    slots = block_values.shape[2]
    group_rows, width = start_panel.shape
    nodes_total = group_rows * lax.axis_size("row") * lax.axis_size("col")
    codes, keeps, lasts = slot_order(block_rows[0, 0], block_cols[0, 0], block_counts[0, 0])
    vmem = pl.BlockSpec(memory_space=pltpu.VMEM)
    smem = pl.BlockSpec(memory_space=pltpu.SMEM)
    panel = jax.ShapeDtypeStruct((group_rows, width), BF16)
    tile = pltpu.VMEM((H, 128, PH, 128), BF16)
    half = pltpu.VMEM((128, PH, 128), BF16)
    turned = jax.ShapeDtypeStruct((width, group_rows), BF16)
    square = jax.ShapeDtypeStruct((width, width), F32)
    mixed = pl.pallas_call(
        functools.partial(kernel, nodes_total),
        out_shape=(turned, turned, square, square),
        in_specs=[smem, smem, smem, vmem, pl.BlockSpec(memory_space=pl.ANY)],
        out_specs=(vmem,) * 4,
        scratch_shapes=[
            pltpu.VMEM((slots, 128, 128), BF16),
            half,
            half,
            pltpu.VMEM((slots + 1, PH, 128), BF16),
            pltpu.VMEM((PH, 128), F32),
            tile,
            tile,
            pltpu.VMEM((H, 2, 2, 8, PH, 128), BF16),
            pltpu.VMEM((H, 2, 2, 16, PH, 128), BF16),
            pltpu.VMEM((H, 2, 3, 4, PH, 128), BF16),
            pltpu.VMEM((H, 2, 4, PH, 128), F32),
            pltpu.VMEM((H, 2, 3, 4, PH, 128), BF16),
            half,
            half,
            pltpu.VMEM((H, 8, 8, PH, 128), BF16),
            pltpu.VMEM((H, 2, 4, 8, PH, 128), BF16),
            pltpu.VMEM((H, 2, 4, 8, PH, 128), BF16),
            pltpu.VMEM((H, 2, 8, PH, 128), F32),
            pltpu.VMEM((128, 1024), F32),
            pltpu.VMEM((2, 128, 128), F32),
            pltpu.VMEM((2, 16, 8, 128), F32),
            pltpu.VMEM((2, 8, 128), F32),
            pltpu.VMEM((2, 16, 8, 128), F32),
            pltpu.VMEM((2, 128, 128), F32),
            pltpu.VMEM((128, 256), F32),
            pltpu.SemaphoreType.DMA,
            pltpu.SemaphoreType.DMA((SENDS,)),
            pltpu.SemaphoreType.DMA((SENDS,)),
        ],
        compiler_params=pltpu.CompilerParams(
            collective_id=0, has_side_effects=True, vmem_limit_bytes=60 * 2**20
        ),
        cost_estimate=pl.CostEstimate(
            flops=4 * slots * 128**3, bytes_accessed=2 * slots * 128 * 128, transcendentals=0
        ),
    )(codes, keeps, lasts, start_panel, block_values[0, 0])
    return pl.pallas_call(apply_kernel, out_shape=(panel, panel), in_specs=[vmem] * 4, out_specs=(vmem, vmem))(*mixed)


def solution(mesh):
    return jax.shard_map(
        local,
        mesh=mesh,
        in_specs=(
            P(("col", "row"), None),
            P("row", "col", None, None, None),
            P("row", "col", None),
            P("row", "col", None),
            P("row", "col"),
        ),
        out_specs=(P(("row", "col"), None), P(("col", "row"), None)),
        check_vma=False,
    )
```

```python
import functools

import jax
import jax.numpy as jnp
from jax import lax
from jax.experimental import pallas as pl
from jax.experimental.pallas import tpu as pltpu
from jax.sharding import PartitionSpec as P

MESH = pl.DeviceIdType.MESH
F32 = jnp.float32
BF16 = jnp.bfloat16
HIGHEST = lax.Precision.HIGHEST

H = 2
PH = 64
UNROLL = 16
PARTS = 4
SENDS = 64
ARRIVALS = 172
GATHER_CUTS = 4
COLUMN_CUTS = 2


class Copies:
    def __init__(self, send_sems, recv_sems):
        self.send_sems, self.recv_sems = send_sems, recv_sems
        self.index, self.sent, self.count = {}, [], 0

    def arrival(self, name):
        number = self.index.setdefault(name, len(self.index))
        assert number < ARRIVALS, number
        return self.recv_sems.at[number]

    def send(self, name, src, dst, device):
        if len(self.sent) == SENDS:
            self.sent.pop(0).wait_send()
        copy = pltpu.make_async_remote_copy(
            src_ref=src,
            dst_ref=dst,
            send_sem=self.send_sems.at[self.count % SENDS],
            recv_sem=self.arrival(name),
            device_id=device,
            device_id_type=MESH,
        )
        self.count += 1
        copy.start()
        self.sent.append(copy)

    def arrived(self, name, dst, device):
        pltpu.make_async_remote_copy(
            src_ref=dst,
            dst_ref=dst,
            send_sem=self.send_sems.at[0],
            recv_sem=self.arrival(name),
            device_id=device,
            device_id_type=MESH,
        ).wait_recv()

    def drain(self):
        for copy in self.sent:
            copy.wait_send()
        self.sent = []


def split3(value):
    high = value.astype(BF16).astype(F32)
    rest = value - high
    middle = rest.astype(BF16).astype(F32)
    return high, middle, (rest - middle).astype(BF16).astype(F32)


def factor_begin(gram, work):
    n = gram.shape[0]
    rows = lax.broadcasted_iota(jnp.int32, (n, n), 0)
    cols = lax.broadcasted_iota(jnp.int32, (n, n), 1)
    work[:, :n] = gram
    work[:, n:] = jnp.where(rows == cols, 1.0, 0.0).astype(F32)


def factor_blocks(work, first, last):
    n = work.shape[0]
    lanes = lax.broadcasted_iota(jnp.int32, (16, n), 1)
    subs = lax.broadcasted_iota(jnp.int32, (8, n), 0)

    def block(jb, carry):
        start = pl.multiple_of(jb * 16, 16)
        rows = work[pl.ds(start, 16), :]
        turned = pltpu.roll(rows[:, :n], lax.rem(n - start, n), 1)
        top = [jnp.broadcast_to(turned[:8, i : i + 1], (8, n)) for i in range(16)]
        low = [jnp.broadcast_to(turned[8:, i : i + 1], (8, n)) for i in range(16)]
        rows_top = [rows[:8, :n], rows[:8, n:]]
        rows_low = [rows[8:, :n], rows[8:, n:]]
        scales = [jnp.zeros((8, n), F32), jnp.zeros((8, n), F32)]
        for i in range(16):
            half, sub = i // 8, i % 8
            source, source_rows = (top, rows_top) if half == 0 else (low, rows_low)
            inverse = jnp.broadcast_to(1.0 / source[i][sub : sub + 1, :], (8, n))
            scales[half] = jnp.where(subs == sub, inverse, scales[half])
            pivots = {j: source[j][sub : sub + 1, :] for j in range(i + 1, 16)}
            pivot_rows = [value[sub : sub + 1, :] for value in source_rows]
            if half == 0:
                factor = jnp.where(subs > sub, top[i] * inverse, 0.0)
                for j in range(i + 1, 16):
                    top[j] = top[j] - factor * pivots[j]
                rows_top = [value - factor * pivot for value, pivot in zip(rows_top, pivot_rows)]
                factor = low[i] * inverse
            else:
                factor = jnp.where(subs > sub, low[i] * inverse, 0.0)
            for j in range(i + 1, 16):
                low[j] = low[j] - factor * pivots[j]
            rows_low = [value - factor * pivot for value, pivot in zip(rows_low, pivot_rows)]
        scale = jnp.concatenate(scales, axis=0)
        d = jnp.concatenate([rows_top[0], rows_low[0]], axis=0)
        m = jnp.concatenate([rows_top[1], rows_low[1]], axis=0)
        left = split3(jnp.where(lanes >= start + 16, d * scale, 0.0))
        right = split3(jnp.concatenate([d, m], axis=1))
        pairs = ((0, 0), (0, 1), (1, 0), (1, 1), (0, 2), (2, 0))
        stacked_left = jnp.concatenate([left[a] for a, _ in pairs], axis=0).T.astype(BF16)
        stacked_right = jnp.concatenate([right[b] for _, b in pairs], axis=0).astype(BF16)
        work[...] = work[...] - jnp.dot(stacked_left, stacked_right, preferred_element_type=F32)
        work[pl.ds(start, 16), n:] = m * jnp.sqrt(scale)
        return carry

    lax.fori_loop(first, last, block, 0)


def kernel(
    nodes_total,
    codes,
    keeps,
    lasts,
    start_ref,
    values_hbm,
    left_y,
    right_y,
    inv1,
    inv2,
    values,
    gathered0,
    gathered1,
    sums,
    run_total,
    partial,
    partial2,
    relay1,
    full1,
    mid,
    mid_own,
    full2,
    left_all0,
    left_all1,
    pair_in,
    ring_out,
    ring_in,
    near_sum,
    z_sum,
    gram_part,
    gram_in1,
    gram_slice,
    gram_in2,
    gram_total,
    work,
    local_sem,
    send_sems,
    recv_sems,
):
    gathered, left_all = (gathered0, gathered1), (left_all0, left_all1)
    slots = values_hbm.shape[0]
    r = lax.axis_index("row")
    c = lax.axis_index("col")
    z, core = r // 2, lax.rem(r, 2)
    position = {"x": c // 4, "y": lax.rem(c, 4)}
    x, y = position["x"], position["y"]
    sibling = {"row": 2 * z + 1 - core}
    z_next = ({"row": lax.rem(r + 2, 16)}, {"row": lax.rem(r + 14, 16)})
    nearby = {
        "x": ({"col": lax.rem(c + 4, 16)}, {"col": lax.rem(c + 12, 16)}),
        "y": ({"col": 4 * x + lax.rem(y + 1, 4)}, {"col": 4 * x + lax.rem(y + 3, 4)}),
    }
    along = {
        "x": [{"col": lax.rem(c + 4 * e, 16)} for e in range(4)],
        "y": [{"col": 4 * x + lax.rem(y + e, 4)} for e in range(4)],
    }
    axes = (("x", "y"), ("y", "x"))
    copies = Copies(send_sems, recv_sems)
    paths = range(2)

    load_values = pltpu.make_async_copy(values_hbm, values, local_sem)
    load_values.start()

    barrier = pltpu.get_barrier_semaphore()
    for t in range(1, 16):
        pl.semaphore_signal(barrier, inc=1, device_id={"row": lax.rem(r + t, 16)}, device_id_type=MESH)
        pl.semaphore_signal(barrier, inc=1, device_id={"col": lax.rem(c + t, 16)}, device_id_type=MESH)

    for b in range(8):
        turned = start_ref[128 * b : 128 * b + 128, :].astype(F32).T.astype(BF16)
        for h in range(H):
            gathered[h][r * 8 + b] = turned[PH * h : PH * h + PH, :]
    sums[slots] = jnp.zeros((PH, 128), BF16)
    pl.semaphore_wait(barrier, 30)

    def group(h, number, first=0, count=8):
        return gathered[h].at[pl.ds(number * 8 + first, count)]

    def origin(way, s):
        return lax.rem(r + (32 - 2 * s if way == 0 else 2 * s), 16)

    cut = 8 // GATHER_CUTS

    def gather_begin(h):
        for q in range(GATHER_CUTS):
            own = group(h, r, cut * q, cut)
            for way in range(2):
                copies.send(("gz", h, way, 1, q), own, own, z_next[way])
        own = group(h, r)
        copies.send(("gs", h), own, own, sibling)

    def last_cuts(way):
        return range(way * GATHER_CUTS // 2, (way + 1) * GATHER_CUTS // 2)

    def gather_step(h, s):
        for q in range(GATHER_CUTS):
            for way in range(2):
                if s == 4 and q not in last_cuts(way):
                    continue
                part = group(h, origin(way, s), cut * q, cut)
                copies.arrived(("gz", h, way, s, q), part, z_next[way])
                if s < 3 or (s == 3 and q in last_cuts(way)):
                    copies.send(("gz", h, way, s + 1, q), part, part, z_next[way])
        for way in range(2):
            whole = group(h, origin(way, s)) if s < 4 else group(h, origin(way, s), 4 * way, 4)
            copies.send(("gs", h), whole, whole, sibling)

    def gather_end(h):
        copies.arrived(("gs", h), gathered[h].at[pl.ds(0, 64)], sibling)

    def product(side, h, part):
        contract = (((1,), (1,)), ((), ())) if side == 0 else (((1,), (0,)), ((), ()))
        panel = gathered[h] if side == 0 else left_all[h]
        steps = slots // UNROLL

        def some_slots(step, total):
            for u in range(UNROLL):
                k = step * UNROLL + u
                code = codes[side * slots + k]
                term = lax.dot_general(panel[code >> 9], values[code & 511], contract, preferred_element_type=F32)
                total = total * keeps[side * slots + k] + term
                sums[k] = total.astype(BF16)
            return total

        total = jnp.zeros((PH, 128), F32) if part == 0 else run_total[...]
        run_total[...] = lax.fori_loop(steps * part // PARTS, steps * (part + 1) // PARTS, some_slots, total)

    def place(side, h):
        out = partial if side == 0 else partial2

        def some_blocks(step, carry):
            for u in range(8):
                q = step * 8 + u
                out[h, q] = sums[lasts[side * 128 + q]]
            return carry

        lax.fori_loop(0, 16, some_blocks, 0)

    def slab(h, path, d1, first=0, count=4):
        return (h, pl.ds(path * 64 + d1 * 16 + first * 4, count * 4))

    def reduce1(h):
        for n in range(2):
            for path in paths:
                axis = axes[path][0]
                far = lax.rem(position[axis] + 2, 4)
                for way in range(2):
                    src = partial.at[slab(h, path, far, 2 * way + n, 1)]
                    dst = relay1.at[h, path, way, pl.ds(4 * n, 4)]
                    copies.send(("r1", h, path, way, n), src, dst, nearby[axis][way])
        for path in paths:
            axis = axes[path][0]
            for way in range(2):
                near = lax.rem(position[axis] + (1 if way == 0 else 3), 4)
                src = partial.at[slab(h, path, near, 2 - 2 * way, 2)]
                dst = full1.at[h, path, way, pl.ds(8 - 8 * way, 8)]
                copies.send(("r1", h, path), src, dst, nearby[axis][way])

    def reduce2(h):
        for n in range(2):
            for path in paths:
                axis = axes[path][0]
                for way in range(2):
                    near = lax.rem(position[axis] + (1 if way == 0 else 3), 4)
                    came = relay1.at[h, path, way, pl.ds(4 * n, 4)]
                    copies.arrived(("r1", h, path, way, n), came, nearby[axis][way])
                    where = slab(h, path, near, 2 * way + n, 1)
                    partial[where] = (partial[where].astype(F32) + came[...].astype(F32)).astype(BF16)
                    dst = full1.at[h, path, way, pl.ds(8 * way + 4 * n, 4)]
                    copies.send(("r1", h, path), partial.at[where], dst, nearby[axis][way])

    def reduce3(h):
        for path in paths:
            axis, other = axes[path]
            m, m2 = position[axis], position[other]
            copies.arrived(("r1", h, path), full1.at[h, path], nearby[axis][0])
            for e in (2, 1, 3, 0):
                d2 = lax.rem(m2 + e, 4)
                total = partial[slab(h, path, m, d2, 1)].astype(F32)
                for way in range(2):
                    total = total + full1[h, path, way, pl.ds(4 * d2, 4)].astype(F32)
                if e == 0:
                    mid_own[h, path] = total
                else:
                    mid[h, path, e - 1] = total.astype(BF16)
                    copies.send(
                        ("r2", h, path), mid.at[h, path, e - 1], full2.at[h, path, e - 1], along[other][e]
                    )

    def piece(h, path, d1, d2, first=0, count=4):
        return left_all[h].at[pl.ds(path * 64 + d1 * 16 + d2 * 4 + first, count)]

    def reduce4(h):
        for path in paths:
            axis, other = axes[path]
            m1, m2 = position[axis], position[other]
            total = mid_own[h, path]
            copies.arrived(("r2", h, path), full2.at[h, path], along[other][1])
            for e in (1, 3, 2):
                total = total + full2[h, path, e - 1].astype(F32)
            rounded = total.astype(BF16)
            left_all[h][pl.ds(path * 64 + m1 * 16 + m2 * 4, 4)] = rounded
            for b in range(4):
                at = 128 * (path * 4 + b)
                left_y[PH * h : PH * h + PH, at : at + 128] = rounded[b]
            own = piece(h, path, m1, m2)
            for e in (2, 1, 3):
                copies.send(("a1", h, path, e), own, own, along[other][e])
            for way in range(2):
                copies.send(("a2", h, path, 0, way, 0), own, own, nearby[axis][way])

    def gram_begin(tag, panel):
        total = lax.dot_general(panel, panel, (((1,), (1,)), ((), ())), preferred_element_type=F32)
        gram_part[tag] = total * (1.0 / nodes_total)
        gram_in1[tag, r] = gram_part[tag, pl.ds(pl.multiple_of(r * 8, 8), 8), :]
        for t in range(1, 16):
            to = lax.rem(r + t, 16)
            src = gram_part.at[tag, pl.ds(pl.multiple_of(to * 8, 8), 8), :]
            copies.send(("m1", tag), src, gram_in1.at[tag, r], {"row": to})

    def gram_middle(tag):
        copies.arrived(("m1", tag), gram_in1.at[tag, pl.ds(0, 15)], sibling)
        gram_slice[tag] = jnp.sum(gram_in1[tag], axis=0)
        gram_in2[tag, c] = gram_slice[tag]
        for t in range(1, 16):
            copies.send(("m2", tag), gram_slice.at[tag], gram_in2.at[tag, c], {"col": lax.rem(c + t, 16)})

    def gram_last(tag):
        copies.arrived(("m2", tag), gram_in2.at[tag, pl.ds(0, 15)], nearby["x"][0])
        mine = gram_total.at[tag, pl.ds(pl.multiple_of(r * 8, 8), 8), :]
        mine[...] = jnp.sum(gram_in2[tag], axis=0)
        for t in range(1, 16):
            copies.send(("m3", tag), mine, mine, {"row": lax.rem(r + t, 16)})

    def gram_end(tag):
        copies.arrived(("m3", tag), gram_total.at[tag, pl.ds(0, 120), :], sibling)

    def second(m2, e):
        return lax.rem(m2 + 4 - e, 4)

    def spread1(h):
        for e in (1, 3, 2):
            for path in paths:
                axis, other = axes[path]
                whole = piece(h, path, position[axis], second(position[other], e))
                copies.arrived(("a1", h, path, e), whole, along[other][e])
                for way in range(2):
                    copies.send(("a2", h, path, e, way, 0), whole, whole, nearby[axis][way])

    def spread3(h, which):
        for path in paths:
            axis, other = axes[path]
            m1, m2 = position[axis], position[other]
            d2 = second(m2, which)
            for way in range(2):
                d1 = lax.rem(m1 + (3 if way == 0 else 1), 4)
                copies.arrived(("a2", h, path, which, way, 0), piece(h, path, d1, d2), nearby[axis][way])
                half = piece(h, path, d1, d2, 2 * way, 2)
                copies.send(("a3", h), half, half, nearby[axis][way])

    def spread_end(h):
        copies.arrived(("a3", h), left_all[h].at[pl.ds(0, 32)], nearby["x"][0])

    def for_z(distance):
        return lax.rem(z + 8 + distance, 8)

    def column0(h):
        for distance in (4, 3, -3, 2, -2, 1, -1, 0):
            src = partial2.at[h, pl.ds((1 - core) * 64 + for_z(distance) * 8, 8)]
            copies.send(("ps", h, distance), src, pair_in.at[h, distance + 3], sibling)

    def pair_sum(h, distance):
        copies.arrived(("ps", h, distance), pair_in.at[h, distance + 3], sibling)
        mine = partial2[h, pl.ds(core * 64 + for_z(distance) * 8, 8)]
        return mine.astype(F32) + pair_in[h, distance + 3].astype(F32)

    span = 8 // COLUMN_CUTS

    def far_cut(way, q):
        return q // (COLUMN_CUTS // 2) == way

    def column_send(h, way, s, q, total):
        at = pl.ds(span * q, span)
        ring_out[h, way, s, at] = total.astype(BF16)
        name = ("rz", h, way, s, q) if s < 3 else ("rz", h)
        copies.send(
            name, ring_out.at[h, way, s, at], ring_in.at[h, way, s, at], z_next[way]
        )

    def column1(h):
        total = pair_sum(h, 4)
        for q in range(COLUMN_CUTS):
            for way in range(2):
                if far_cut(way, q):
                    column_send(h, way, 0, q, total[span * q : span * q + span])
        for way in range(2):
            total = pair_sum(h, 3 - 6 * way)
            near_sum[h, way] = total
            for q in range(COLUMN_CUTS):
                if not far_cut(way, q):
                    column_send(h, way, 1, q, total[span * q : span * q + span])

    def column2(h, s):
        if s > 1:
            for way in range(2):
                near_sum[h, way] = pair_sum(h, (4 - s) * (1 - 2 * way))
        for first in (True, False):
            for q in range(COLUMN_CUTS):
                for way in range(2):
                    far = far_cut(way, q)
                    if far == first or (s == 1 and not far):
                        continue
                    at = pl.ds(span * q, span)
                    came = ring_in.at[h, way, s - 1, at]
                    copies.arrived(("rz", h, way, s - 1, q), came, z_next[way])
                    column_send(h, way, s, q, near_sum[h, way, at] + came[...].astype(F32))

    def column3(h):
        total = pair_sum(h, 0)
        copies.arrived(("rz", h), ring_in.at[h, 0, pl.ds(0, 2)], z_next[0])
        for way in range(2):
            total = total + ring_in[h, way, 3].astype(F32)
        for b in range(8):
            z_sum[PH * h : PH * h + PH, 128 * b : 128 * b + 128] = total[b]

    gather_begin(0)
    gather_step(0, 1)
    gather_begin(1)
    for s in (2, 3):
        gather_step(0, s)
        gather_step(1, s - 1)
    gather_step(0, 4)
    gather_end(0)
    load_values.wait()
    product(0, 0, 0)
    gather_step(1, 3)
    product(0, 0, 1)
    product(0, 0, 2)
    gather_step(1, 4)
    product(0, 0, 3)
    place(0, 0)
    reduce1(0)
    gather_end(1)
    product(0, 1, 0)
    product(0, 1, 1)
    reduce2(0)
    product(0, 1, 2)
    product(0, 1, 3)
    place(0, 1)
    reduce1(1)
    reduce3(0)
    reduce2(1)
    reduce4(0)
    reduce3(1)
    spread1(0)
    spread3(0, 0)
    reduce4(1)
    gram_begin(0, left_y[...])
    spread3(0, 1)
    spread3(0, 3)
    spread3(0, 2)
    spread1(1)
    spread_end(0)
    product(1, 0, 0)
    spread3(1, 0)
    product(1, 0, 1)
    spread3(1, 1)
    spread3(1, 3)
    product(1, 0, 2)
    spread3(1, 2)
    product(1, 0, 3)
    place(1, 0)
    column0(0)
    gram_middle(0)
    column1(0)
    spread_end(1)
    product(1, 1, 0)
    product(1, 1, 1)
    column2(0, 1)
    gram_last(0)
    product(1, 1, 2)
    product(1, 1, 3)
    place(1, 1)
    column0(1)
    column2(0, 2)
    column1(1)
    gram_end(0)
    factor_begin(gram_total[0], work)
    factor_blocks(work, 0, 2)
    column2(0, 3)
    column2(1, 1)
    factor_blocks(work, 2, 4)
    column3(0)
    column2(1, 2)
    factor_blocks(work, 4, 6)
    column2(1, 3)
    factor_blocks(work, 6, 8)
    inv1[...] = work[:, 128:]
    column3(1)
    right_sum = jnp.dot(inv1[...], z_sum[...], precision=HIGHEST, preferred_element_type=F32)
    right_y[...] = right_sum.astype(BF16)
    gram_begin(1, right_y[...])
    gram_middle(1)
    gram_last(1)
    gram_end(1)
    factor_begin(gram_total[1], work)
    factor_blocks(work, 0, 8)
    inv2[...] = work[:, 128:]
    copies.drain()


def apply_kernel(left_y, right_y, inv1, inv2, left_out, right_out):
    for y, inverse, out in ((left_y, inv1, left_out), (right_y, inv2, right_out)):
        parts = split3(inverse[...])
        total = sum(jnp.dot(part.astype(BF16), y[...], preferred_element_type=F32) for part in parts[::-1])
        for b in range(8):
            out[128 * b : 128 * b + 128, :] = total[:, 128 * b : 128 * b + 128].T.astype(BF16)


def slot_order(rows, cols, count):
    slots = rows.shape[0]
    number = jnp.arange(slots, dtype=jnp.int32)
    live = number < count
    group, b = rows // 8, rows % 8
    gx, gy = group // 4, group % 4
    path, blk = b // 4, b % 4
    row_place = path * 64 + jnp.where(path == 0, gx * 16 + gy * 4, gy * 16 + gx * 4) + blk
    key = jnp.where(live[None, :], jnp.stack([rows, cols]), 128)
    inputs = jnp.stack([cols, row_place])
    packed = number[None, :] + 512 * inputs + 65536 * key
    ahead = (key[:, None, :] < key[:, :, None]) | (
        (key[:, None, :] == key[:, :, None]) & (number[None, None, :] < number[None, :, None])
    )
    rank = jnp.sum(ahead.astype(jnp.int32), axis=2)
    hit = rank[:, :, None] == number[None, None, :]
    in_order = jnp.sum(jnp.where(hit, packed[:, :, None], 0), axis=1)
    codes = in_order & 65535
    key_order = in_order >> 16
    keeps = jnp.concatenate(
        [jnp.zeros((2, 1), F32), (key_order[:, 1:] == key_order[:, :-1]).astype(F32)], axis=1
    )
    q = jnp.arange(128, dtype=jnp.int32)
    path, d1, d2, blk = q // 64, q // 16 % 4, q // 4 % 4, q % 4
    left_block = jnp.where(path == 0, d1 * 4 + d2, d2 * 4 + d1) * 8 + path * 4 + blk
    right_block = (2 * (q // 8 % 8) + q // 64) * 8 + q % 8
    block = jnp.stack([left_block, right_block])
    upto = jnp.sum((key[:, :, None] <= block[:, None, :]).astype(jnp.int32), axis=1)
    below = jnp.sum((key[:, :, None] < block[:, None, :]).astype(jnp.int32), axis=1)
    lasts = jnp.where(upto > below, upto - 1, slots)
    return codes.reshape(-1), keeps.reshape(-1), lasts.reshape(-1)


def local(start_panel, block_values, block_rows, block_cols, block_counts):
    slots = block_values.shape[2]
    group_rows, width = start_panel.shape
    nodes_total = group_rows * lax.axis_size("row") * lax.axis_size("col")
    codes, keeps, lasts = slot_order(block_rows[0, 0], block_cols[0, 0], block_counts[0, 0])
    vmem = pl.BlockSpec(memory_space=pltpu.VMEM)
    smem = pl.BlockSpec(memory_space=pltpu.SMEM)
    panel = jax.ShapeDtypeStruct((group_rows, width), BF16)
    tile = pltpu.VMEM((H, 128, PH, 128), BF16)
    half = pltpu.VMEM((128, PH, 128), BF16)
    turned = jax.ShapeDtypeStruct((width, group_rows), BF16)
    square = jax.ShapeDtypeStruct((width, width), F32)
    mixed = pl.pallas_call(
        functools.partial(kernel, nodes_total),
        out_shape=(turned, turned, square, square),
        in_specs=[smem, smem, smem, vmem, pl.BlockSpec(memory_space=pl.ANY)],
        out_specs=(vmem,) * 4,
        scratch_shapes=[
            pltpu.VMEM((slots, 128, 128), BF16),
            half,
            half,
            pltpu.VMEM((slots + 1, PH, 128), BF16),
            pltpu.VMEM((PH, 128), F32),
            tile,
            tile,
            pltpu.VMEM((H, 2, 2, 8, PH, 128), BF16),
            pltpu.VMEM((H, 2, 2, 16, PH, 128), BF16),
            pltpu.VMEM((H, 2, 3, 4, PH, 128), BF16),
            pltpu.VMEM((H, 2, 4, PH, 128), F32),
            pltpu.VMEM((H, 2, 3, 4, PH, 128), BF16),
            half,
            half,
            pltpu.VMEM((H, 8, 8, PH, 128), BF16),
            pltpu.VMEM((H, 2, 4, 8, PH, 128), BF16),
            pltpu.VMEM((H, 2, 4, 8, PH, 128), BF16),
            pltpu.VMEM((H, 2, 8, PH, 128), F32),
            pltpu.VMEM((128, 1024), F32),
            pltpu.VMEM((2, 128, 128), F32),
            pltpu.VMEM((2, 16, 8, 128), F32),
            pltpu.VMEM((2, 8, 128), F32),
            pltpu.VMEM((2, 16, 8, 128), F32),
            pltpu.VMEM((2, 128, 128), F32),
            pltpu.VMEM((128, 256), F32),
            pltpu.SemaphoreType.DMA,
            pltpu.SemaphoreType.DMA((SENDS,)),
            pltpu.SemaphoreType.DMA((ARRIVALS,)),
        ],
        compiler_params=pltpu.CompilerParams(
            collective_id=0, has_side_effects=True, vmem_limit_bytes=60 * 2**20
        ),
        cost_estimate=pl.CostEstimate(
            flops=4 * slots * 128**3, bytes_accessed=2 * slots * 128 * 128, transcendentals=0
        ),
    )(codes, keeps, lasts, start_panel, block_values[0, 0])
    return pl.pallas_call(apply_kernel, out_shape=(panel, panel), in_specs=[vmem] * 4, out_specs=(vmem, vmem))(*mixed)


def solution(mesh):
    return jax.shard_map(
        local,
        mesh=mesh,
        in_specs=(
            P(("col", "row"), None),
            P("row", "col", None, None, None),
            P("row", "col", None),
            P("row", "col", None),
            P("row", "col"),
        ),
        out_specs=(P(("row", "col"), None), P(("col", "row"), None)),
        check_vma=False,
    )
```

```python
import functools

import jax
import jax.numpy as jnp
from jax import lax
from jax.experimental import pallas as pl
from jax.experimental.pallas import tpu as pltpu
from jax.sharding import PartitionSpec as P

MESH = pl.DeviceIdType.MESH
F32 = jnp.float32
BF16 = jnp.bfloat16
HIGHEST = lax.Precision.HIGHEST

H = 2
PH = 64
UNROLL = 32
PARTS = 4
SENDS = 64
ARRIVALS = 172
GATHER_CUTS = 4
COLUMN_CUTS = 2


class Copies:
    def __init__(self, send_sems, recv_sems):
        self.send_sems, self.recv_sems = send_sems, recv_sems
        self.index, self.sent, self.count = {}, [], 0

    def arrival(self, name):
        number = self.index.setdefault(name, len(self.index))
        assert number < ARRIVALS, number
        return self.recv_sems.at[number]

    def send(self, name, src, dst, device):
        if len(self.sent) == SENDS:
            self.sent.pop(0).wait_send()
        copy = pltpu.make_async_remote_copy(
            src_ref=src,
            dst_ref=dst,
            send_sem=self.send_sems.at[self.count % SENDS],
            recv_sem=self.arrival(name),
            device_id=device,
            device_id_type=MESH,
        )
        self.count += 1
        copy.start()
        self.sent.append(copy)

    def arrived(self, name, dst, device):
        pltpu.make_async_remote_copy(
            src_ref=dst,
            dst_ref=dst,
            send_sem=self.send_sems.at[0],
            recv_sem=self.arrival(name),
            device_id=device,
            device_id_type=MESH,
        ).wait_recv()

    def drain(self):
        for copy in self.sent:
            copy.wait_send()
        self.sent = []


def split3(value):
    high = value.astype(BF16).astype(F32)
    rest = value - high
    middle = rest.astype(BF16).astype(F32)
    return high, middle, (rest - middle).astype(BF16).astype(F32)


def factor_begin(gram, work):
    n = gram.shape[0]
    rows = lax.broadcasted_iota(jnp.int32, (n, n), 0)
    cols = lax.broadcasted_iota(jnp.int32, (n, n), 1)
    work[:, :n] = gram
    work[:, n:] = jnp.where(rows == cols, 1.0, 0.0).astype(F32)


def factor_blocks(work, first, last):
    n = work.shape[0]
    lanes = lax.broadcasted_iota(jnp.int32, (16, n), 1)
    subs = lax.broadcasted_iota(jnp.int32, (8, n), 0)

    def block(jb, carry):
        start = pl.multiple_of(jb * 16, 16)
        rows = work[pl.ds(start, 16), :]
        turned = pltpu.roll(rows[:, :n], lax.rem(n - start, n), 1)
        top = [jnp.broadcast_to(turned[:8, i : i + 1], (8, n)) for i in range(16)]
        low = [jnp.broadcast_to(turned[8:, i : i + 1], (8, n)) for i in range(16)]
        rows_top = [rows[:8, :n], rows[:8, n:]]
        rows_low = [rows[8:, :n], rows[8:, n:]]
        scales = [jnp.zeros((8, n), F32), jnp.zeros((8, n), F32)]
        for i in range(16):
            half, sub = i // 8, i % 8
            source, source_rows = (top, rows_top) if half == 0 else (low, rows_low)
            inverse = jnp.broadcast_to(1.0 / source[i][sub : sub + 1, :], (8, n))
            scales[half] = jnp.where(subs == sub, inverse, scales[half])
            pivots = {j: source[j][sub : sub + 1, :] for j in range(i + 1, 16)}
            pivot_rows = [value[sub : sub + 1, :] for value in source_rows]
            if half == 0:
                factor = jnp.where(subs > sub, top[i] * inverse, 0.0)
                for j in range(i + 1, 16):
                    top[j] = top[j] - factor * pivots[j]
                rows_top = [value - factor * pivot for value, pivot in zip(rows_top, pivot_rows)]
                factor = low[i] * inverse
            else:
                factor = jnp.where(subs > sub, low[i] * inverse, 0.0)
            for j in range(i + 1, 16):
                low[j] = low[j] - factor * pivots[j]
            rows_low = [value - factor * pivot for value, pivot in zip(rows_low, pivot_rows)]
        scale = jnp.concatenate(scales, axis=0)
        d = jnp.concatenate([rows_top[0], rows_low[0]], axis=0)
        m = jnp.concatenate([rows_top[1], rows_low[1]], axis=0)
        left = split3(jnp.where(lanes >= start + 16, d * scale, 0.0))
        right = split3(jnp.concatenate([d, m], axis=1))
        pairs = ((0, 0), (0, 1), (1, 0), (1, 1), (0, 2), (2, 0))
        stacked_left = jnp.concatenate([left[a] for a, _ in pairs], axis=0).T.astype(BF16)
        stacked_right = jnp.concatenate([right[b] for _, b in pairs], axis=0).astype(BF16)
        work[...] = work[...] - jnp.dot(stacked_left, stacked_right, preferred_element_type=F32)
        work[pl.ds(start, 16), n:] = m * jnp.sqrt(scale)
        return carry

    lax.fori_loop(first, last, block, 0)


def kernel(
    nodes_total,
    codes,
    keeps,
    lasts,
    start_ref,
    values_hbm,
    left_y,
    right_y,
    inv1,
    inv2,
    values,
    gathered0,
    gathered1,
    sums,
    run_total,
    partial,
    partial2,
    relay1,
    full1,
    mid,
    mid_own,
    full2,
    left_all0,
    left_all1,
    pair_in,
    ring_out,
    ring_in,
    near_sum,
    z_sum,
    gram_part,
    gram_in1,
    gram_slice,
    gram_in2,
    gram_total,
    work,
    local_sem,
    send_sems,
    recv_sems,
):
    gathered, left_all = (gathered0, gathered1), (left_all0, left_all1)
    slots = values_hbm.shape[0]
    r = lax.axis_index("row")
    c = lax.axis_index("col")
    z, core = r // 2, lax.rem(r, 2)
    position = {"x": c // 4, "y": lax.rem(c, 4)}
    x, y = position["x"], position["y"]
    sibling = {"row": 2 * z + 1 - core}
    z_next = ({"row": lax.rem(r + 2, 16)}, {"row": lax.rem(r + 14, 16)})
    nearby = {
        "x": ({"col": lax.rem(c + 4, 16)}, {"col": lax.rem(c + 12, 16)}),
        "y": ({"col": 4 * x + lax.rem(y + 1, 4)}, {"col": 4 * x + lax.rem(y + 3, 4)}),
    }
    along = {
        "x": [{"col": lax.rem(c + 4 * e, 16)} for e in range(4)],
        "y": [{"col": 4 * x + lax.rem(y + e, 4)} for e in range(4)],
    }
    axes = (("x", "y"), ("y", "x"))
    copies = Copies(send_sems, recv_sems)
    paths = range(2)

    load_values = pltpu.make_async_copy(values_hbm, values, local_sem)
    load_values.start()

    barrier = pltpu.get_barrier_semaphore()
    for t in range(1, 16):
        pl.semaphore_signal(barrier, inc=1, device_id={"row": lax.rem(r + t, 16)}, device_id_type=MESH)
        pl.semaphore_signal(barrier, inc=1, device_id={"col": lax.rem(c + t, 16)}, device_id_type=MESH)

    for b in range(8):
        turned = start_ref[128 * b : 128 * b + 128, :].astype(F32).T.astype(BF16)
        for h in range(H):
            gathered[h][r * 8 + b] = turned[PH * h : PH * h + PH, :]
    sums[slots] = jnp.zeros((PH, 128), BF16)
    pl.semaphore_wait(barrier, 30)

    def group(h, number, first=0, count=8):
        return gathered[h].at[pl.ds(number * 8 + first, count)]

    def origin(way, s):
        return lax.rem(r + (32 - 2 * s if way == 0 else 2 * s), 16)

    cut = 8 // GATHER_CUTS

    def gather_begin(h):
        for q in range(GATHER_CUTS):
            own = group(h, r, cut * q, cut)
            for way in range(2):
                copies.send(("gz", h, way, 1, q), own, own, z_next[way])
        own = group(h, r)
        copies.send(("gs", h), own, own, sibling)

    def last_cuts(way):
        return range(way * GATHER_CUTS // 2, (way + 1) * GATHER_CUTS // 2)

    def gather_step(h, s):
        for q in range(GATHER_CUTS):
            for way in range(2):
                if s == 4 and q not in last_cuts(way):
                    continue
                part = group(h, origin(way, s), cut * q, cut)
                copies.arrived(("gz", h, way, s, q), part, z_next[way])
                if s < 3 or (s == 3 and q in last_cuts(way)):
                    copies.send(("gz", h, way, s + 1, q), part, part, z_next[way])
        for way in range(2):
            whole = group(h, origin(way, s)) if s < 4 else group(h, origin(way, s), 4 * way, 4)
            copies.send(("gs", h), whole, whole, sibling)

    def gather_end(h):
        copies.arrived(("gs", h), gathered[h].at[pl.ds(0, 64)], sibling)

    def product(side, h, part):
        contract = (((1,), (1,)), ((), ())) if side == 0 else (((1,), (0,)), ((), ()))
        panel = gathered[h] if side == 0 else left_all[h]
        steps = slots // UNROLL

        def some_slots(step, total):
            for u in range(UNROLL):
                k = step * UNROLL + u
                code = codes[side * slots + k]
                term = lax.dot_general(panel[code >> 9], values[code & 511], contract, preferred_element_type=F32)
                total = total * keeps[side * slots + k] + term
                sums[k] = total.astype(BF16)
            return total

        total = jnp.zeros((PH, 128), F32) if part == 0 else run_total[...]
        run_total[...] = lax.fori_loop(steps * part // PARTS, steps * (part + 1) // PARTS, some_slots, total)

    def place(side, h):
        out = partial if side == 0 else partial2

        def some_blocks(step, carry):
            for u in range(8):
                q = step * 8 + u
                out[h, q] = sums[lasts[side * 128 + q]]
            return carry

        lax.fori_loop(0, 16, some_blocks, 0)

    def slab(h, path, d1, first=0, count=4):
        return (h, pl.ds(path * 64 + d1 * 16 + first * 4, count * 4))

    def reduce1(h):
        for n in range(2):
            for path in paths:
                axis = axes[path][0]
                far = lax.rem(position[axis] + 2, 4)
                for way in range(2):
                    src = partial.at[slab(h, path, far, 2 * way + n, 1)]
                    dst = relay1.at[h, path, way, pl.ds(4 * n, 4)]
                    copies.send(("r1", h, path, way, n), src, dst, nearby[axis][way])
        for path in paths:
            axis = axes[path][0]
            for way in range(2):
                near = lax.rem(position[axis] + (1 if way == 0 else 3), 4)
                src = partial.at[slab(h, path, near, 2 - 2 * way, 2)]
                dst = full1.at[h, path, way, pl.ds(8 - 8 * way, 8)]
                copies.send(("r1", h, path), src, dst, nearby[axis][way])

    def reduce2(h):
        for n in range(2):
            for path in paths:
                axis = axes[path][0]
                for way in range(2):
                    near = lax.rem(position[axis] + (1 if way == 0 else 3), 4)
                    came = relay1.at[h, path, way, pl.ds(4 * n, 4)]
                    copies.arrived(("r1", h, path, way, n), came, nearby[axis][way])
                    where = slab(h, path, near, 2 * way + n, 1)
                    partial[where] = (partial[where].astype(F32) + came[...].astype(F32)).astype(BF16)
                    dst = full1.at[h, path, way, pl.ds(8 * way + 4 * n, 4)]
                    copies.send(("r1", h, path), partial.at[where], dst, nearby[axis][way])

    def reduce3(h):
        for path in paths:
            axis, other = axes[path]
            m, m2 = position[axis], position[other]
            copies.arrived(("r1", h, path), full1.at[h, path], nearby[axis][0])
            for e in (2, 1, 3, 0):
                d2 = lax.rem(m2 + e, 4)
                total = partial[slab(h, path, m, d2, 1)].astype(F32)
                for way in range(2):
                    total = total + full1[h, path, way, pl.ds(4 * d2, 4)].astype(F32)
                if e == 0:
                    mid_own[h, path] = total
                else:
                    mid[h, path, e - 1] = total.astype(BF16)
                    copies.send(
                        ("r2", h, path), mid.at[h, path, e - 1], full2.at[h, path, e - 1], along[other][e]
                    )

    def piece(h, path, d1, d2, first=0, count=4):
        return left_all[h].at[pl.ds(path * 64 + d1 * 16 + d2 * 4 + first, count)]

    def reduce4(h):
        for path in paths:
            axis, other = axes[path]
            m1, m2 = position[axis], position[other]
            total = mid_own[h, path]
            copies.arrived(("r2", h, path), full2.at[h, path], along[other][1])
            for e in (1, 3, 2):
                total = total + full2[h, path, e - 1].astype(F32)
            rounded = total.astype(BF16)
            left_all[h][pl.ds(path * 64 + m1 * 16 + m2 * 4, 4)] = rounded
            for b in range(4):
                at = 128 * (path * 4 + b)
                left_y[PH * h : PH * h + PH, at : at + 128] = rounded[b]
            own = piece(h, path, m1, m2)
            for e in (2, 1, 3):
                copies.send(("a1", h, path, e), own, own, along[other][e])
            for way in range(2):
                copies.send(("a2", h, path, 0, way, 0), own, own, nearby[axis][way])

    def gram_begin(tag, panel):
        total = lax.dot_general(panel, panel, (((1,), (1,)), ((), ())), preferred_element_type=F32)
        gram_part[tag] = total * (1.0 / nodes_total)
        gram_in1[tag, r] = gram_part[tag, pl.ds(pl.multiple_of(r * 8, 8), 8), :]
        for t in range(1, 16):
            to = lax.rem(r + t, 16)
            src = gram_part.at[tag, pl.ds(pl.multiple_of(to * 8, 8), 8), :]
            copies.send(("m1", tag), src, gram_in1.at[tag, r], {"row": to})

    def gram_middle(tag):
        copies.arrived(("m1", tag), gram_in1.at[tag, pl.ds(0, 15)], sibling)
        gram_slice[tag] = jnp.sum(gram_in1[tag], axis=0)
        gram_in2[tag, c] = gram_slice[tag]
        for t in range(1, 16):
            copies.send(("m2", tag), gram_slice.at[tag], gram_in2.at[tag, c], {"col": lax.rem(c + t, 16)})

    def gram_last(tag):
        copies.arrived(("m2", tag), gram_in2.at[tag, pl.ds(0, 15)], nearby["x"][0])
        mine = gram_total.at[tag, pl.ds(pl.multiple_of(r * 8, 8), 8), :]
        mine[...] = jnp.sum(gram_in2[tag], axis=0)
        for t in range(1, 16):
            copies.send(("m3", tag), mine, mine, {"row": lax.rem(r + t, 16)})

    def gram_end(tag):
        copies.arrived(("m3", tag), gram_total.at[tag, pl.ds(0, 120), :], sibling)

    def second(m2, e):
        return lax.rem(m2 + 4 - e, 4)

    def spread1(h):
        for e in (1, 3, 2):
            for path in paths:
                axis, other = axes[path]
                whole = piece(h, path, position[axis], second(position[other], e))
                copies.arrived(("a1", h, path, e), whole, along[other][e])
                for way in range(2):
                    copies.send(("a2", h, path, e, way, 0), whole, whole, nearby[axis][way])

    def spread3(h, which):
        for path in paths:
            axis, other = axes[path]
            m1, m2 = position[axis], position[other]
            d2 = second(m2, which)
            for way in range(2):
                d1 = lax.rem(m1 + (3 if way == 0 else 1), 4)
                copies.arrived(("a2", h, path, which, way, 0), piece(h, path, d1, d2), nearby[axis][way])
                half = piece(h, path, d1, d2, 2 * way, 2)
                copies.send(("a3", h), half, half, nearby[axis][way])

    def spread_end(h):
        copies.arrived(("a3", h), left_all[h].at[pl.ds(0, 32)], nearby["x"][0])

    def for_z(distance):
        return lax.rem(z + 8 + distance, 8)

    def column0(h):
        for distance in (4, 3, -3, 2, -2, 1, -1, 0):
            src = partial2.at[h, pl.ds((1 - core) * 64 + for_z(distance) * 8, 8)]
            copies.send(("ps", h, distance), src, pair_in.at[h, distance + 3], sibling)

    def pair_sum(h, distance):
        copies.arrived(("ps", h, distance), pair_in.at[h, distance + 3], sibling)
        mine = partial2[h, pl.ds(core * 64 + for_z(distance) * 8, 8)]
        return mine.astype(F32) + pair_in[h, distance + 3].astype(F32)

    span = 8 // COLUMN_CUTS

    def far_cut(way, q):
        return q // (COLUMN_CUTS // 2) == way

    def column_send(h, way, s, q, total):
        at = pl.ds(span * q, span)
        ring_out[h, way, s, at] = total.astype(BF16)
        name = ("rz", h, way, s, q) if s < 3 else ("rz", h)
        copies.send(
            name, ring_out.at[h, way, s, at], ring_in.at[h, way, s, at], z_next[way]
        )

    def column1(h):
        total = pair_sum(h, 4)
        for q in range(COLUMN_CUTS):
            for way in range(2):
                if far_cut(way, q):
                    column_send(h, way, 0, q, total[span * q : span * q + span])
        for way in range(2):
            total = pair_sum(h, 3 - 6 * way)
            near_sum[h, way] = total
            for q in range(COLUMN_CUTS):
                if not far_cut(way, q):
                    column_send(h, way, 1, q, total[span * q : span * q + span])

    def column2(h, s):
        if s > 1:
            for way in range(2):
                near_sum[h, way] = pair_sum(h, (4 - s) * (1 - 2 * way))
        for first in (True, False):
            for q in range(COLUMN_CUTS):
                for way in range(2):
                    far = far_cut(way, q)
                    if far == first or (s == 1 and not far):
                        continue
                    at = pl.ds(span * q, span)
                    came = ring_in.at[h, way, s - 1, at]
                    copies.arrived(("rz", h, way, s - 1, q), came, z_next[way])
                    column_send(h, way, s, q, near_sum[h, way, at] + came[...].astype(F32))

    def column3(h):
        total = pair_sum(h, 0)
        copies.arrived(("rz", h), ring_in.at[h, 0, pl.ds(0, 2)], z_next[0])
        for way in range(2):
            total = total + ring_in[h, way, 3].astype(F32)
        for b in range(8):
            z_sum[PH * h : PH * h + PH, 128 * b : 128 * b + 128] = total[b]

    gather_begin(0)
    gather_step(0, 1)
    gather_begin(1)
    for s in (2, 3):
        gather_step(0, s)
        gather_step(1, s - 1)
    gather_step(0, 4)
    gather_end(0)
    load_values.wait()
    product(0, 0, 0)
    gather_step(1, 3)
    product(0, 0, 1)
    product(0, 0, 2)
    gather_step(1, 4)
    product(0, 0, 3)
    place(0, 0)
    reduce1(0)
    gather_end(1)
    product(0, 1, 0)
    product(0, 1, 1)
    reduce2(0)
    product(0, 1, 2)
    product(0, 1, 3)
    place(0, 1)
    reduce1(1)
    reduce3(0)
    reduce2(1)
    reduce4(0)
    reduce3(1)
    spread1(0)
    spread3(0, 0)
    reduce4(1)
    gram_begin(0, left_y[...])
    spread3(0, 1)
    spread3(0, 3)
    spread3(0, 2)
    spread1(1)
    spread_end(0)
    product(1, 0, 0)
    spread3(1, 0)
    product(1, 0, 1)
    spread3(1, 1)
    spread3(1, 3)
    product(1, 0, 2)
    spread3(1, 2)
    product(1, 0, 3)
    place(1, 0)
    column0(0)
    gram_middle(0)
    column1(0)
    spread_end(1)
    product(1, 1, 0)
    product(1, 1, 1)
    column2(0, 1)
    gram_last(0)
    product(1, 1, 2)
    product(1, 1, 3)
    place(1, 1)
    column0(1)
    column2(0, 2)
    column1(1)
    gram_end(0)
    factor_begin(gram_total[0], work)
    factor_blocks(work, 0, 2)
    column2(0, 3)
    column2(1, 1)
    factor_blocks(work, 2, 4)
    column3(0)
    column2(1, 2)
    factor_blocks(work, 4, 6)
    column2(1, 3)
    factor_blocks(work, 6, 8)
    inv1[...] = work[:, 128:]
    column3(1)
    right_sum = jnp.dot(inv1[...], z_sum[...], precision=HIGHEST, preferred_element_type=F32)
    right_y[...] = right_sum.astype(BF16)
    gram_begin(1, right_y[...])
    gram_middle(1)
    gram_last(1)
    gram_end(1)
    factor_begin(gram_total[1], work)
    factor_blocks(work, 0, 8)
    inv2[...] = work[:, 128:]
    copies.drain()


def apply_kernel(left_y, right_y, inv1, inv2, left_out, right_out):
    for y, inverse, out in ((left_y, inv1, left_out), (right_y, inv2, right_out)):
        parts = split3(inverse[...])
        total = sum(jnp.dot(part.astype(BF16), y[...], preferred_element_type=F32) for part in parts[::-1])
        for b in range(8):
            out[128 * b : 128 * b + 128, :] = total[:, 128 * b : 128 * b + 128].T.astype(BF16)


def slot_order(rows, cols, count):
    slots = rows.shape[0]
    number = jnp.arange(slots, dtype=jnp.int32)
    live = number < count
    group, b = rows // 8, rows % 8
    gx, gy = group // 4, group % 4
    path, blk = b // 4, b % 4
    row_place = path * 64 + jnp.where(path == 0, gx * 16 + gy * 4, gy * 16 + gx * 4) + blk
    key = jnp.where(live[None, :], jnp.stack([rows, cols]), 128)
    inputs = jnp.stack([cols, row_place])
    packed = number[None, :] + 512 * inputs + 65536 * key
    ahead = (key[:, None, :] < key[:, :, None]) | (
        (key[:, None, :] == key[:, :, None]) & (number[None, None, :] < number[None, :, None])
    )
    rank = jnp.sum(ahead.astype(jnp.int32), axis=2)
    hit = rank[:, :, None] == number[None, None, :]
    in_order = jnp.sum(jnp.where(hit, packed[:, :, None], 0), axis=1)
    codes = in_order & 65535
    key_order = in_order >> 16
    keeps = jnp.concatenate(
        [jnp.zeros((2, 1), F32), (key_order[:, 1:] == key_order[:, :-1]).astype(F32)], axis=1
    )
    q = jnp.arange(128, dtype=jnp.int32)
    path, d1, d2, blk = q // 64, q // 16 % 4, q // 4 % 4, q % 4
    left_block = jnp.where(path == 0, d1 * 4 + d2, d2 * 4 + d1) * 8 + path * 4 + blk
    right_block = (2 * (q // 8 % 8) + q // 64) * 8 + q % 8
    block = jnp.stack([left_block, right_block])
    upto = jnp.sum((key[:, :, None] <= block[:, None, :]).astype(jnp.int32), axis=1)
    below = jnp.sum((key[:, :, None] < block[:, None, :]).astype(jnp.int32), axis=1)
    lasts = jnp.where(upto > below, upto - 1, slots)
    return codes.reshape(-1), keeps.reshape(-1), lasts.reshape(-1)


def local(start_panel, block_values, block_rows, block_cols, block_counts):
    slots = block_values.shape[2]
    group_rows, width = start_panel.shape
    nodes_total = group_rows * lax.axis_size("row") * lax.axis_size("col")
    codes, keeps, lasts = slot_order(block_rows[0, 0], block_cols[0, 0], block_counts[0, 0])
    vmem = pl.BlockSpec(memory_space=pltpu.VMEM)
    smem = pl.BlockSpec(memory_space=pltpu.SMEM)
    panel = jax.ShapeDtypeStruct((group_rows, width), BF16)
    tile = pltpu.VMEM((H, 128, PH, 128), BF16)
    half = pltpu.VMEM((128, PH, 128), BF16)
    turned = jax.ShapeDtypeStruct((width, group_rows), BF16)
    square = jax.ShapeDtypeStruct((width, width), F32)
    mixed = pl.pallas_call(
        functools.partial(kernel, nodes_total),
        out_shape=(turned, turned, square, square),
        in_specs=[smem, smem, smem, vmem, pl.BlockSpec(memory_space=pl.ANY)],
        out_specs=(vmem,) * 4,
        scratch_shapes=[
            pltpu.VMEM((slots, 128, 128), BF16),
            half,
            half,
            pltpu.VMEM((slots + 1, PH, 128), BF16),
            pltpu.VMEM((PH, 128), F32),
            tile,
            tile,
            pltpu.VMEM((H, 2, 2, 8, PH, 128), BF16),
            pltpu.VMEM((H, 2, 2, 16, PH, 128), BF16),
            pltpu.VMEM((H, 2, 3, 4, PH, 128), BF16),
            pltpu.VMEM((H, 2, 4, PH, 128), F32),
            pltpu.VMEM((H, 2, 3, 4, PH, 128), BF16),
            half,
            half,
            pltpu.VMEM((H, 8, 8, PH, 128), BF16),
            pltpu.VMEM((H, 2, 4, 8, PH, 128), BF16),
            pltpu.VMEM((H, 2, 4, 8, PH, 128), BF16),
            pltpu.VMEM((H, 2, 8, PH, 128), F32),
            pltpu.VMEM((128, 1024), F32),
            pltpu.VMEM((2, 128, 128), F32),
            pltpu.VMEM((2, 16, 8, 128), F32),
            pltpu.VMEM((2, 8, 128), F32),
            pltpu.VMEM((2, 16, 8, 128), F32),
            pltpu.VMEM((2, 128, 128), F32),
            pltpu.VMEM((128, 256), F32),
            pltpu.SemaphoreType.DMA,
            pltpu.SemaphoreType.DMA((SENDS,)),
            pltpu.SemaphoreType.DMA((ARRIVALS,)),
        ],
        compiler_params=pltpu.CompilerParams(
            collective_id=0, has_side_effects=True, vmem_limit_bytes=60 * 2**20
        ),
        cost_estimate=pl.CostEstimate(
            flops=4 * slots * 128**3, bytes_accessed=2 * slots * 128 * 128, transcendentals=0
        ),
    )(codes, keeps, lasts, start_panel, block_values[0, 0])
    return pl.pallas_call(apply_kernel, out_shape=(panel, panel), in_specs=[vmem] * 4, out_specs=(vmem, vmem))(*mixed)


def solution(mesh):
    return jax.shard_map(
        local,
        mesh=mesh,
        in_specs=(
            P(("col", "row"), None),
            P("row", "col", None, None, None),
            P("row", "col", None),
            P("row", "col", None),
            P("row", "col"),
        ),
        out_specs=(P(("row", "col"), None), P(("col", "row"), None)),
        check_vma=False,
    )
```

```python
import functools

import jax
import jax.numpy as jnp
from jax import lax
from jax.experimental import pallas as pl
from jax.experimental.pallas import tpu as pltpu
from jax.sharding import PartitionSpec as P

MESH = pl.DeviceIdType.MESH
F32 = jnp.float32
BF16 = jnp.bfloat16
HIGHEST = lax.Precision.HIGHEST

H = 2
PH = 64
UNROLL = 44
PARTS = 4
SENDS = 64
ARRIVALS = 172
GATHER_CUTS = 4
COLUMN_CUTS = 2


class Copies:
    def __init__(self, send_sems, recv_sems):
        self.send_sems, self.recv_sems = send_sems, recv_sems
        self.index, self.sent, self.count = {}, [], 0

    def arrival(self, name):
        number = self.index.setdefault(name, len(self.index))
        assert number < ARRIVALS, number
        return self.recv_sems.at[number]

    def send(self, name, src, dst, device):
        if len(self.sent) == SENDS:
            self.sent.pop(0).wait_send()
        copy = pltpu.make_async_remote_copy(
            src_ref=src,
            dst_ref=dst,
            send_sem=self.send_sems.at[self.count % SENDS],
            recv_sem=self.arrival(name),
            device_id=device,
            device_id_type=MESH,
        )
        self.count += 1
        copy.start()
        self.sent.append(copy)

    def arrived(self, name, dst, device):
        pltpu.make_async_remote_copy(
            src_ref=dst,
            dst_ref=dst,
            send_sem=self.send_sems.at[0],
            recv_sem=self.arrival(name),
            device_id=device,
            device_id_type=MESH,
        ).wait_recv()

    def drain(self):
        for copy in self.sent:
            copy.wait_send()
        self.sent = []


def split3(value):
    high = value.astype(BF16).astype(F32)
    rest = value - high
    middle = rest.astype(BF16).astype(F32)
    return high, middle, (rest - middle).astype(BF16).astype(F32)


def factor_begin(gram, work):
    n = gram.shape[0]
    rows = lax.broadcasted_iota(jnp.int32, (n, n), 0)
    cols = lax.broadcasted_iota(jnp.int32, (n, n), 1)
    work[:, :n] = gram
    work[:, n:] = jnp.where(rows == cols, 1.0, 0.0).astype(F32)


def factor_blocks(work, first, last):
    n = work.shape[0]
    lanes = lax.broadcasted_iota(jnp.int32, (16, n), 1)
    subs = lax.broadcasted_iota(jnp.int32, (8, n), 0)

    def block(jb, carry):
        start = pl.multiple_of(jb * 16, 16)
        rows = work[pl.ds(start, 16), :]
        turned = pltpu.roll(rows[:, :n], lax.rem(n - start, n), 1)
        top = [jnp.broadcast_to(turned[:8, i : i + 1], (8, n)) for i in range(16)]
        low = [jnp.broadcast_to(turned[8:, i : i + 1], (8, n)) for i in range(16)]
        rows_top = [rows[:8, :n], rows[:8, n:]]
        rows_low = [rows[8:, :n], rows[8:, n:]]
        scales = [jnp.zeros((8, n), F32), jnp.zeros((8, n), F32)]
        for i in range(16):
            half, sub = i // 8, i % 8
            source, source_rows = (top, rows_top) if half == 0 else (low, rows_low)
            inverse = jnp.broadcast_to(1.0 / source[i][sub : sub + 1, :], (8, n))
            scales[half] = jnp.where(subs == sub, inverse, scales[half])
            pivots = {j: source[j][sub : sub + 1, :] for j in range(i + 1, 16)}
            pivot_rows = [value[sub : sub + 1, :] for value in source_rows]
            if half == 0:
                factor = jnp.where(subs > sub, top[i] * inverse, 0.0)
                for j in range(i + 1, 16):
                    top[j] = top[j] - factor * pivots[j]
                rows_top = [value - factor * pivot for value, pivot in zip(rows_top, pivot_rows)]
                factor = low[i] * inverse
            else:
                factor = jnp.where(subs > sub, low[i] * inverse, 0.0)
            for j in range(i + 1, 16):
                low[j] = low[j] - factor * pivots[j]
            rows_low = [value - factor * pivot for value, pivot in zip(rows_low, pivot_rows)]
        scale = jnp.concatenate(scales, axis=0)
        d = jnp.concatenate([rows_top[0], rows_low[0]], axis=0)
        m = jnp.concatenate([rows_top[1], rows_low[1]], axis=0)
        left = split3(jnp.where(lanes >= start + 16, d * scale, 0.0))
        right = split3(jnp.concatenate([d, m], axis=1))
        pairs = ((0, 0), (0, 1), (1, 0), (1, 1), (0, 2), (2, 0))
        stacked_left = jnp.concatenate([left[a] for a, _ in pairs], axis=0).T.astype(BF16)
        stacked_right = jnp.concatenate([right[b] for _, b in pairs], axis=0).astype(BF16)
        work[...] = work[...] - jnp.dot(stacked_left, stacked_right, preferred_element_type=F32)
        work[pl.ds(start, 16), n:] = m * jnp.sqrt(scale)
        return carry

    lax.fori_loop(first, last, block, 0)


def kernel(
    nodes_total,
    codes,
    keeps,
    lasts,
    start_ref,
    values_hbm,
    left_y,
    right_y,
    inv1,
    inv2,
    values,
    gathered0,
    gathered1,
    sums,
    run_total,
    partial,
    partial2,
    relay1,
    full1,
    mid,
    mid_own,
    full2,
    left_all0,
    left_all1,
    pair_in,
    ring_out,
    ring_in,
    near_sum,
    z_sum,
    gram_part,
    gram_in1,
    gram_slice,
    gram_in2,
    gram_total,
    work,
    local_sem,
    send_sems,
    recv_sems,
):
    gathered, left_all = (gathered0, gathered1), (left_all0, left_all1)
    slots = values_hbm.shape[0]
    r = lax.axis_index("row")
    c = lax.axis_index("col")
    z, core = r // 2, lax.rem(r, 2)
    position = {"x": c // 4, "y": lax.rem(c, 4)}
    x, y = position["x"], position["y"]
    sibling = {"row": 2 * z + 1 - core}
    z_next = ({"row": lax.rem(r + 2, 16)}, {"row": lax.rem(r + 14, 16)})
    nearby = {
        "x": ({"col": lax.rem(c + 4, 16)}, {"col": lax.rem(c + 12, 16)}),
        "y": ({"col": 4 * x + lax.rem(y + 1, 4)}, {"col": 4 * x + lax.rem(y + 3, 4)}),
    }
    along = {
        "x": [{"col": lax.rem(c + 4 * e, 16)} for e in range(4)],
        "y": [{"col": 4 * x + lax.rem(y + e, 4)} for e in range(4)],
    }
    axes = (("x", "y"), ("y", "x"))
    copies = Copies(send_sems, recv_sems)
    paths = range(2)

    load_values = pltpu.make_async_copy(values_hbm, values, local_sem)
    load_values.start()

    barrier = pltpu.get_barrier_semaphore()
    for t in range(1, 16):
        pl.semaphore_signal(barrier, inc=1, device_id={"row": lax.rem(r + t, 16)}, device_id_type=MESH)
        pl.semaphore_signal(barrier, inc=1, device_id={"col": lax.rem(c + t, 16)}, device_id_type=MESH)

    for b in range(8):
        turned = start_ref[128 * b : 128 * b + 128, :].astype(F32).T.astype(BF16)
        for h in range(H):
            gathered[h][r * 8 + b] = turned[PH * h : PH * h + PH, :]
    sums[slots] = jnp.zeros((PH, 128), BF16)
    pl.semaphore_wait(barrier, 30)

    def group(h, number, first=0, count=8):
        return gathered[h].at[pl.ds(number * 8 + first, count)]

    def origin(way, s):
        return lax.rem(r + (32 - 2 * s if way == 0 else 2 * s), 16)

    cut = 8 // GATHER_CUTS

    def gather_begin(h):
        for q in range(GATHER_CUTS):
            own = group(h, r, cut * q, cut)
            for way in range(2):
                copies.send(("gz", h, way, 1, q), own, own, z_next[way])
        own = group(h, r)
        copies.send(("gs", h), own, own, sibling)

    def last_cuts(way):
        return range(way * GATHER_CUTS // 2, (way + 1) * GATHER_CUTS // 2)

    def gather_step(h, s):
        for q in range(GATHER_CUTS):
            for way in range(2):
                if s == 4 and q not in last_cuts(way):
                    continue
                part = group(h, origin(way, s), cut * q, cut)
                copies.arrived(("gz", h, way, s, q), part, z_next[way])
                if s < 3 or (s == 3 and q in last_cuts(way)):
                    copies.send(("gz", h, way, s + 1, q), part, part, z_next[way])
        for way in range(2):
            whole = group(h, origin(way, s)) if s < 4 else group(h, origin(way, s), 4 * way, 4)
            copies.send(("gs", h), whole, whole, sibling)

    def gather_end(h):
        copies.arrived(("gs", h), gathered[h].at[pl.ds(0, 64)], sibling)

    def product(side, h, part):
        contract = (((1,), (1,)), ((), ())) if side == 0 else (((1,), (0,)), ((), ()))
        panel = gathered[h] if side == 0 else left_all[h]
        steps = slots // UNROLL

        def some_slots(step, total):
            for u in range(UNROLL):
                k = step * UNROLL + u
                code = codes[side * slots + k]
                term = lax.dot_general(panel[code >> 9], values[code & 511], contract, preferred_element_type=F32)
                total = total * keeps[side * slots + k] + term
                sums[k] = total.astype(BF16)
            return total

        total = jnp.zeros((PH, 128), F32) if part == 0 else run_total[...]
        run_total[...] = lax.fori_loop(steps * part // PARTS, steps * (part + 1) // PARTS, some_slots, total)

    def place(side, h):
        out = partial if side == 0 else partial2

        def some_blocks(step, carry):
            for u in range(8):
                q = step * 8 + u
                out[h, q] = sums[lasts[side * 128 + q]]
            return carry

        lax.fori_loop(0, 16, some_blocks, 0)

    def slab(h, path, d1, first=0, count=4):
        return (h, pl.ds(path * 64 + d1 * 16 + first * 4, count * 4))

    def reduce1(h):
        for n in range(2):
            for path in paths:
                axis = axes[path][0]
                far = lax.rem(position[axis] + 2, 4)
                for way in range(2):
                    src = partial.at[slab(h, path, far, 2 * way + n, 1)]
                    dst = relay1.at[h, path, way, pl.ds(4 * n, 4)]
                    copies.send(("r1", h, path, way, n), src, dst, nearby[axis][way])
        for path in paths:
            axis = axes[path][0]
            for way in range(2):
                near = lax.rem(position[axis] + (1 if way == 0 else 3), 4)
                src = partial.at[slab(h, path, near, 2 - 2 * way, 2)]
                dst = full1.at[h, path, way, pl.ds(8 - 8 * way, 8)]
                copies.send(("r1", h, path), src, dst, nearby[axis][way])

    def reduce2(h):
        for n in range(2):
            for path in paths:
                axis = axes[path][0]
                for way in range(2):
                    near = lax.rem(position[axis] + (1 if way == 0 else 3), 4)
                    came = relay1.at[h, path, way, pl.ds(4 * n, 4)]
                    copies.arrived(("r1", h, path, way, n), came, nearby[axis][way])
                    where = slab(h, path, near, 2 * way + n, 1)
                    partial[where] = (partial[where].astype(F32) + came[...].astype(F32)).astype(BF16)
                    dst = full1.at[h, path, way, pl.ds(8 * way + 4 * n, 4)]
                    copies.send(("r1", h, path), partial.at[where], dst, nearby[axis][way])

    def reduce3(h):
        for path in paths:
            axis, other = axes[path]
            m, m2 = position[axis], position[other]
            copies.arrived(("r1", h, path), full1.at[h, path], nearby[axis][0])
            for e in (2, 1, 3, 0):
                d2 = lax.rem(m2 + e, 4)
                total = partial[slab(h, path, m, d2, 1)].astype(F32)
                for way in range(2):
                    total = total + full1[h, path, way, pl.ds(4 * d2, 4)].astype(F32)
                if e == 0:
                    mid_own[h, path] = total
                else:
                    mid[h, path, e - 1] = total.astype(BF16)
                    copies.send(
                        ("r2", h, path), mid.at[h, path, e - 1], full2.at[h, path, e - 1], along[other][e]
                    )

    def piece(h, path, d1, d2, first=0, count=4):
        return left_all[h].at[pl.ds(path * 64 + d1 * 16 + d2 * 4 + first, count)]

    def reduce4(h):
        for path in paths:
            axis, other = axes[path]
            m1, m2 = position[axis], position[other]
            total = mid_own[h, path]
            copies.arrived(("r2", h, path), full2.at[h, path], along[other][1])
            for e in (1, 3, 2):
                total = total + full2[h, path, e - 1].astype(F32)
            rounded = total.astype(BF16)
            left_all[h][pl.ds(path * 64 + m1 * 16 + m2 * 4, 4)] = rounded
            for b in range(4):
                at = 128 * (path * 4 + b)
                left_y[PH * h : PH * h + PH, at : at + 128] = rounded[b]
            own = piece(h, path, m1, m2)
            for e in (2, 1, 3):
                copies.send(("a1", h, path, e), own, own, along[other][e])
            for way in range(2):
                copies.send(("a2", h, path, 0, way, 0), own, own, nearby[axis][way])

    def gram_begin(tag, panel):
        total = lax.dot_general(panel, panel, (((1,), (1,)), ((), ())), preferred_element_type=F32)
        gram_part[tag] = total * (1.0 / nodes_total)
        gram_in1[tag, r] = gram_part[tag, pl.ds(pl.multiple_of(r * 8, 8), 8), :]
        for t in range(1, 16):
            to = lax.rem(r + t, 16)
            src = gram_part.at[tag, pl.ds(pl.multiple_of(to * 8, 8), 8), :]
            copies.send(("m1", tag), src, gram_in1.at[tag, r], {"row": to})

    def gram_middle(tag):
        copies.arrived(("m1", tag), gram_in1.at[tag, pl.ds(0, 15)], sibling)
        gram_slice[tag] = jnp.sum(gram_in1[tag], axis=0)
        gram_in2[tag, c] = gram_slice[tag]
        for t in range(1, 16):
            copies.send(("m2", tag), gram_slice.at[tag], gram_in2.at[tag, c], {"col": lax.rem(c + t, 16)})

    def gram_last(tag):
        copies.arrived(("m2", tag), gram_in2.at[tag, pl.ds(0, 15)], nearby["x"][0])
        mine = gram_total.at[tag, pl.ds(pl.multiple_of(r * 8, 8), 8), :]
        mine[...] = jnp.sum(gram_in2[tag], axis=0)
        for t in range(1, 16):
            copies.send(("m3", tag), mine, mine, {"row": lax.rem(r + t, 16)})

    def gram_end(tag):
        copies.arrived(("m3", tag), gram_total.at[tag, pl.ds(0, 120), :], sibling)

    def second(m2, e):
        return lax.rem(m2 + 4 - e, 4)

    def spread1(h):
        for e in (1, 3, 2):
            for path in paths:
                axis, other = axes[path]
                whole = piece(h, path, position[axis], second(position[other], e))
                copies.arrived(("a1", h, path, e), whole, along[other][e])
                for way in range(2):
                    copies.send(("a2", h, path, e, way, 0), whole, whole, nearby[axis][way])

    def spread3(h, which):
        for path in paths:
            axis, other = axes[path]
            m1, m2 = position[axis], position[other]
            d2 = second(m2, which)
            for way in range(2):
                d1 = lax.rem(m1 + (3 if way == 0 else 1), 4)
                copies.arrived(("a2", h, path, which, way, 0), piece(h, path, d1, d2), nearby[axis][way])
                half = piece(h, path, d1, d2, 2 * way, 2)
                copies.send(("a3", h), half, half, nearby[axis][way])

    def spread_end(h):
        copies.arrived(("a3", h), left_all[h].at[pl.ds(0, 32)], nearby["x"][0])

    def for_z(distance):
        return lax.rem(z + 8 + distance, 8)

    def column0(h):
        for distance in (4, 3, -3, 2, -2, 1, -1, 0):
            src = partial2.at[h, pl.ds((1 - core) * 64 + for_z(distance) * 8, 8)]
            copies.send(("ps", h, distance), src, pair_in.at[h, distance + 3], sibling)

    def pair_sum(h, distance):
        copies.arrived(("ps", h, distance), pair_in.at[h, distance + 3], sibling)
        mine = partial2[h, pl.ds(core * 64 + for_z(distance) * 8, 8)]
        return mine.astype(F32) + pair_in[h, distance + 3].astype(F32)

    span = 8 // COLUMN_CUTS

    def far_cut(way, q):
        return q // (COLUMN_CUTS // 2) == way

    def column_send(h, way, s, q, total):
        at = pl.ds(span * q, span)
        ring_out[h, way, s, at] = total.astype(BF16)
        name = ("rz", h, way, s, q) if s < 3 else ("rz", h)
        copies.send(
            name, ring_out.at[h, way, s, at], ring_in.at[h, way, s, at], z_next[way]
        )

    def column1(h):
        total = pair_sum(h, 4)
        for q in range(COLUMN_CUTS):
            for way in range(2):
                if far_cut(way, q):
                    column_send(h, way, 0, q, total[span * q : span * q + span])
        for way in range(2):
            total = pair_sum(h, 3 - 6 * way)
            near_sum[h, way] = total
            for q in range(COLUMN_CUTS):
                if not far_cut(way, q):
                    column_send(h, way, 1, q, total[span * q : span * q + span])

    def column2(h, s):
        if s > 1:
            for way in range(2):
                near_sum[h, way] = pair_sum(h, (4 - s) * (1 - 2 * way))
        for first in (True, False):
            for q in range(COLUMN_CUTS):
                for way in range(2):
                    far = far_cut(way, q)
                    if far == first or (s == 1 and not far):
                        continue
                    at = pl.ds(span * q, span)
                    came = ring_in.at[h, way, s - 1, at]
                    copies.arrived(("rz", h, way, s - 1, q), came, z_next[way])
                    column_send(h, way, s, q, near_sum[h, way, at] + came[...].astype(F32))

    def column3(h):
        total = pair_sum(h, 0)
        copies.arrived(("rz", h), ring_in.at[h, 0, pl.ds(0, 2)], z_next[0])
        for way in range(2):
            total = total + ring_in[h, way, 3].astype(F32)
        for b in range(8):
            z_sum[PH * h : PH * h + PH, 128 * b : 128 * b + 128] = total[b]

    gather_begin(0)
    gather_step(0, 1)
    gather_begin(1)
    for s in (2, 3):
        gather_step(0, s)
        gather_step(1, s - 1)
    gather_step(0, 4)
    gather_end(0)
    load_values.wait()
    product(0, 0, 0)
    gather_step(1, 3)
    product(0, 0, 1)
    product(0, 0, 2)
    gather_step(1, 4)
    product(0, 0, 3)
    place(0, 0)
    reduce1(0)
    gather_end(1)
    product(0, 1, 0)
    product(0, 1, 1)
    reduce2(0)
    product(0, 1, 2)
    product(0, 1, 3)
    place(0, 1)
    reduce1(1)
    reduce3(0)
    reduce2(1)
    reduce4(0)
    reduce3(1)
    spread1(0)
    spread3(0, 0)
    reduce4(1)
    gram_begin(0, left_y[...])
    spread3(0, 1)
    spread3(0, 3)
    spread3(0, 2)
    spread1(1)
    spread_end(0)
    product(1, 0, 0)
    spread3(1, 0)
    product(1, 0, 1)
    spread3(1, 1)
    spread3(1, 3)
    product(1, 0, 2)
    spread3(1, 2)
    product(1, 0, 3)
    place(1, 0)
    column0(0)
    gram_middle(0)
    column1(0)
    spread_end(1)
    product(1, 1, 0)
    product(1, 1, 1)
    column2(0, 1)
    gram_last(0)
    product(1, 1, 2)
    product(1, 1, 3)
    place(1, 1)
    column0(1)
    column2(0, 2)
    column1(1)
    gram_end(0)
    factor_begin(gram_total[0], work)
    factor_blocks(work, 0, 2)
    column2(0, 3)
    column2(1, 1)
    factor_blocks(work, 2, 4)
    column3(0)
    column2(1, 2)
    factor_blocks(work, 4, 6)
    column2(1, 3)
    factor_blocks(work, 6, 8)
    inv1[...] = work[:, 128:]
    column3(1)
    right_sum = jnp.dot(inv1[...], z_sum[...], precision=HIGHEST, preferred_element_type=F32)
    right_y[...] = right_sum.astype(BF16)
    gram_begin(1, right_y[...])
    gram_middle(1)
    gram_last(1)
    gram_end(1)
    factor_begin(gram_total[1], work)
    factor_blocks(work, 0, 8)
    inv2[...] = work[:, 128:]
    copies.drain()


def apply_kernel(left_y, right_y, inv1, inv2, left_out, right_out):
    for y, inverse, out in ((left_y, inv1, left_out), (right_y, inv2, right_out)):
        parts = split3(inverse[...])
        total = sum(jnp.dot(part.astype(BF16), y[...], preferred_element_type=F32) for part in parts[::-1])
        for b in range(8):
            out[128 * b : 128 * b + 128, :] = total[:, 128 * b : 128 * b + 128].T.astype(BF16)


def slot_order(rows, cols, count):
    slots = rows.shape[0]
    number = jnp.arange(slots, dtype=jnp.int32)
    live = number < count
    group, b = rows // 8, rows % 8
    gx, gy = group // 4, group % 4
    path, blk = b // 4, b % 4
    row_place = path * 64 + jnp.where(path == 0, gx * 16 + gy * 4, gy * 16 + gx * 4) + blk
    key = jnp.where(live[None, :], jnp.stack([rows, cols]), 128)
    inputs = jnp.stack([cols, row_place])
    packed = number[None, :] + 512 * inputs + 65536 * key
    ahead = (key[:, None, :] < key[:, :, None]) | (
        (key[:, None, :] == key[:, :, None]) & (number[None, None, :] < number[None, :, None])
    )
    rank = jnp.sum(ahead.astype(jnp.int32), axis=2)
    hit = rank[:, :, None] == number[None, None, :]
    in_order = jnp.sum(jnp.where(hit, packed[:, :, None], 0), axis=1)
    codes = in_order & 65535
    key_order = in_order >> 16
    keeps = jnp.concatenate(
        [jnp.zeros((2, 1), F32), (key_order[:, 1:] == key_order[:, :-1]).astype(F32)], axis=1
    )
    q = jnp.arange(128, dtype=jnp.int32)
    path, d1, d2, blk = q // 64, q // 16 % 4, q // 4 % 4, q % 4
    left_block = jnp.where(path == 0, d1 * 4 + d2, d2 * 4 + d1) * 8 + path * 4 + blk
    right_block = (2 * (q // 8 % 8) + q // 64) * 8 + q % 8
    block = jnp.stack([left_block, right_block])
    upto = jnp.sum((key[:, :, None] <= block[:, None, :]).astype(jnp.int32), axis=1)
    below = jnp.sum((key[:, :, None] < block[:, None, :]).astype(jnp.int32), axis=1)
    lasts = jnp.where(upto > below, upto - 1, slots)
    return codes.reshape(-1), keeps.reshape(-1), lasts.reshape(-1)


def local(start_panel, block_values, block_rows, block_cols, block_counts):
    slots = block_values.shape[2]
    group_rows, width = start_panel.shape
    nodes_total = group_rows * lax.axis_size("row") * lax.axis_size("col")
    codes, keeps, lasts = slot_order(block_rows[0, 0], block_cols[0, 0], block_counts[0, 0])
    vmem = pl.BlockSpec(memory_space=pltpu.VMEM)
    smem = pl.BlockSpec(memory_space=pltpu.SMEM)
    panel = jax.ShapeDtypeStruct((group_rows, width), BF16)
    tile = pltpu.VMEM((H, 128, PH, 128), BF16)
    half = pltpu.VMEM((128, PH, 128), BF16)
    turned = jax.ShapeDtypeStruct((width, group_rows), BF16)
    square = jax.ShapeDtypeStruct((width, width), F32)
    mixed = pl.pallas_call(
        functools.partial(kernel, nodes_total),
        out_shape=(turned, turned, square, square),
        in_specs=[smem, smem, smem, vmem, pl.BlockSpec(memory_space=pl.ANY)],
        out_specs=(vmem,) * 4,
        scratch_shapes=[
            pltpu.VMEM((slots, 128, 128), BF16),
            half,
            half,
            pltpu.VMEM((slots + 1, PH, 128), BF16),
            pltpu.VMEM((PH, 128), F32),
            tile,
            tile,
            pltpu.VMEM((H, 2, 2, 8, PH, 128), BF16),
            pltpu.VMEM((H, 2, 2, 16, PH, 128), BF16),
            pltpu.VMEM((H, 2, 3, 4, PH, 128), BF16),
            pltpu.VMEM((H, 2, 4, PH, 128), F32),
            pltpu.VMEM((H, 2, 3, 4, PH, 128), BF16),
            half,
            half,
            pltpu.VMEM((H, 8, 8, PH, 128), BF16),
            pltpu.VMEM((H, 2, 4, 8, PH, 128), BF16),
            pltpu.VMEM((H, 2, 4, 8, PH, 128), BF16),
            pltpu.VMEM((H, 2, 8, PH, 128), F32),
            pltpu.VMEM((128, 1024), F32),
            pltpu.VMEM((2, 128, 128), F32),
            pltpu.VMEM((2, 16, 8, 128), F32),
            pltpu.VMEM((2, 8, 128), F32),
            pltpu.VMEM((2, 16, 8, 128), F32),
            pltpu.VMEM((2, 128, 128), F32),
            pltpu.VMEM((128, 256), F32),
            pltpu.SemaphoreType.DMA,
            pltpu.SemaphoreType.DMA((SENDS,)),
            pltpu.SemaphoreType.DMA((ARRIVALS,)),
        ],
        compiler_params=pltpu.CompilerParams(
            collective_id=0, has_side_effects=True, vmem_limit_bytes=60 * 2**20
        ),
        cost_estimate=pl.CostEstimate(
            flops=4 * slots * 128**3, bytes_accessed=2 * slots * 128 * 128, transcendentals=0
        ),
    )(codes, keeps, lasts, start_panel, block_values[0, 0])
    return pl.pallas_call(apply_kernel, out_shape=(panel, panel), in_specs=[vmem] * 4, out_specs=(vmem, vmem))(*mixed)


def solution(mesh):
    return jax.shard_map(
        local,
        mesh=mesh,
        in_specs=(
            P(("col", "row"), None),
            P("row", "col", None, None, None),
            P("row", "col", None),
            P("row", "col", None),
            P("row", "col"),
        ),
        out_specs=(P(("row", "col"), None), P(("col", "row"), None)),
        check_vma=False,
    )
```
